32 devices in a mesh: plane: 16 (over z, y, x), cuts: 2 (over core).
Axes of the slice: x: 2, y: 2, z: 4, core: 2. Of those that a mesh axis runs over, the one named last changes fastest.
Arguments:
- image: float32 [256, 128, 256], P('plane', None, 'cuts'), may hold values from 0 to 2
- projection_weight_tiles: bfloat16 [1536, 256, 256], P('plane'), may hold values from -0.0390625 to 0.0390625
- pair_tile_index: int32 [1536], P('plane'), may hold values from 0 to 7
- pair_ray_block: int32 [1536], P('plane'), may hold values from 0 to 15
- ray_owner: int32 [16], replicated, may hold values from 0 to 15, each once
- active_pair_count: int32 [16], P('plane'), may hold values from 12 to 96, as said below
- measured: float32 [16, 256, 256], P('plane', None, 'cuts'), may hold values from -6 to 6
Outputs:
- volume: float32 [256, 128, 256], P('plane', None, 'cuts')
- residual: bfloat16 [16, 256, 256], P('plane', None, 'cuts')
The draws below stay inside these ranges and needn't reach their ends.
Inputs may be any that keep to these rules, and one draw needn't show every extreme that they name: The first active_pair_count[d] pairs of plane index d are live and the rest are not; some index has all 96 pairs live. `ray_owner`: each owner position is taken by exactly one ray block.
All inputs are finite; a program needn't handle non-finite values.
Results may differ from the reference program's by a relative error of at most 0.0045.
Values may be sent and summed in bfloat16 or wider, within the bound.
No kernel may reach another device: no remote copies, remote signals or barrier semaphores. Data moves between devices by JAX's collectives and lax.ppermute only.
A program may use at most 128 MiB of HBM per device.

```python
import jax
import jax.numpy as jnp
from jax import lax

TILE = 16
RAYS_PER_BLOCK = 256
COLS = 128
PAIRS_PER_PLANE = 96
SWEEPS = 4
NDEV = 16
TILE_VOXELS = 256
NY = 256
SLICES = 256
TILES_PER_PLANE = 8
NTILES = 128
RAY_BLOCK_TOTAL = 16
PAIR_TOTAL = 1536


def draw_active_pair_count(key, part):
    first_key = jax.random.fold_in(key, 11)
    second_key = jax.random.fold_in(key, 23)
    counts_drawn = jax.random.randint(first_key, (NDEV,), PAIRS_PER_PLANE // 8, PAIRS_PER_PLANE + 1)
    busiest = jax.random.randint(second_key, (), 0, NDEV)
    return jnp.where(jnp.arange(NDEV) == busiest, PAIRS_PER_PLANE, counts_drawn).astype(jnp.int32)


def with_ends(drawn, key, low, high):
    longest = drawn.shape.index(max(drawn.shape))
    spots = []
    for shift in (0, 1):
        where = [jax.random.randint(jax.random.fold_in(key, axis), (), 0, length) for axis, length in enumerate(drawn.shape)]
        where[longest] = (where[longest] + shift) % drawn.shape[longest]
        spots.append(tuple(where))
    return drawn.at[spots[0]].set(low).at[spots[1]].set(high)


def levels(rng, shape, cuts, least, top_value):
    gain = 1.0
    for dim, parts in cuts:
        heights = jax.random.uniform(jax.random.fold_in(jax.random.fold_in(rng, 6), dim), (parts,), jnp.float32, least / len(cuts), top_value / len(cuts))
        gain = gain * jnp.repeat(jnp.exp(heights), shape[dim] // parts).reshape((-1,) + (1,) * (len(shape) - 1 - dim))
    return gain


def scatter_about(rng, shape, scale, most, shards=(), kind=jnp.bfloat16):
    gain = levels(rng, shape, shards, -0.22, 0.18) if shards else 1.0
    values = jax.random.normal(rng, shape, jnp.float32) * scale * gain
    return jnp.minimum(jnp.maximum(values, -most), most).astype(kind)


def setup_inputs(seed: int = 0) -> dict:
    arg_keys = jax.random.split(jax.random.key(seed), 8)
    return {
        "image": jnp.clip(2.0 * jax.random.uniform(arg_keys[0], (NY, COLS, SLICES), jnp.float32) ** levels(arg_keys[0], (NY, COLS, SLICES), ((0, 16), (2, 2)), -0.2, 0.2), 0.0, 2.0),
        "projection_weight_tiles": scatter_about(arg_keys[1], (PAIR_TOTAL, TILE_VOXELS, RAYS_PER_BLOCK), (TILE_VOXELS * PAIRS_PER_PLANE) ** -0.5, 0.0390625, ((0, 16),)),
        "pair_tile_index": with_ends(jax.random.randint(arg_keys[2], (PAIR_TOTAL,), 0, TILES_PER_PLANE), jax.random.fold_in(arg_keys[2], 1), 0, TILES_PER_PLANE - 1).astype(jnp.int32),
        "pair_ray_block": with_ends(jax.random.randint(arg_keys[3], (PAIR_TOTAL,), 0, RAY_BLOCK_TOTAL), jax.random.fold_in(arg_keys[3], 1), 0, RAY_BLOCK_TOTAL - 1).astype(jnp.int32),
        "ray_owner": jax.random.permutation(arg_keys[4], RAY_BLOCK_TOTAL).astype(jnp.int32),
        "active_pair_count": draw_active_pair_count(jax.random.fold_in(arg_keys[7], 71), 0),
        "measured": scatter_about(arg_keys[6], (RAY_BLOCK_TOTAL, RAYS_PER_BLOCK, SLICES), 1.0, 6.0, ((0, 16), (2, 2)), jnp.float32),
    }


smooth_square = 0.09
flow_step = 0.04
relax_step = 4.0

def smooth_sweep(volume, inside):
    rise_rows = jnp.concatenate([volume[1:] - volume[:-1], -volume[-1:]], axis=0)
    rise_cols = jnp.concatenate([volume[:, 1:] - volume[:, :-1], -volume[:, -1:]], axis=1)
    rise_slices = jnp.concatenate([volume[:, :, 1:] - volume[:, :, :-1], -volume[:, :, -1:]], axis=2)
    length = jnp.sqrt(smooth_square + rise_rows * rise_rows + rise_cols * rise_cols + rise_slices * rise_slices)
    flow_rows = rise_rows / length * inside
    flow_cols = rise_cols / length * inside
    flow_slices = rise_slices / length * inside
    diverge = flow_rows - jnp.concatenate([jnp.zeros_like(flow_rows[:1]), flow_rows[:-1]], axis=0)
    diverge = diverge + flow_cols - jnp.concatenate([jnp.zeros_like(flow_cols[:, :1]), flow_cols[:, :-1]], axis=1)
    diverge = diverge + flow_slices - jnp.concatenate([jnp.zeros_like(flow_slices[:, :, :1]), flow_slices[:, :, :-1]], axis=2)
    return (volume + flow_step * diverge) * inside

def reference(image, projection_weight_tiles, pair_tile_index, pair_ray_block, ray_owner, active_pair_count, measured):
    grouped = image.reshape(NY // TILE, TILE, COLS // TILE, TILE, SLICES).transpose(0, 2, 1, 3, 4).reshape(NTILES, TILE_VOXELS, SLICES)
    rounded = lax.optimization_barrier(grouped.astype(jnp.bfloat16)).astype(jnp.float32)
    plane_index_of = (jnp.arange(PAIR_TOTAL, dtype=jnp.int32) // PAIRS_PER_PLANE).astype(jnp.int32)
    owner_of = ray_owner[pair_ray_block].astype(jnp.int32)
    active_pair = (jnp.arange(PAIR_TOTAL, dtype=jnp.int32) % PAIRS_PER_PLANE < active_pair_count[plane_index_of]).astype(jnp.float32)
    stacked = (projection_weight_tiles.reshape(NDEV, PAIRS_PER_PLANE, TILE_VOXELS, RAYS_PER_BLOCK), pair_tile_index.reshape(NDEV, PAIRS_PER_PLANE), owner_of.reshape(NDEV, PAIRS_PER_PLANE), active_pair.reshape(NDEV, PAIRS_PER_PLANE), rounded.reshape(NDEV, TILES_PER_PLANE, TILE_VOXELS, SLICES))

    def forward(running, pieces):
        weights, tile_ids, owners, live_part, local_tiles = pieces
        values = local_tiles[tile_ids]
        product = jnp.einsum('svr,svc->src', weights.astype(jnp.float32), values, precision=lax.Precision.HIGHEST)
        product = product * live_part[:, None, None]
        return (running + jax.ops.segment_sum(product, owners, num_segments=RAY_BLOCK_TOTAL), None)
    projection, unused = lax.scan(forward, jnp.zeros((RAY_BLOCK_TOTAL, RAYS_PER_BLOCK, SLICES), jnp.float32), stacked)
    mismatch = measured - projection
    residual = (mismatch / jnp.sqrt(1.0 + mismatch * mismatch)).astype(jnp.bfloat16)
    residual_wide = residual.astype(jnp.float32)

    def backward(carry, pieces):
        weights, tile_ids, owners, live_part, local_tiles = pieces
        product = jnp.einsum('svr,src->svc', weights.astype(jnp.float32), residual_wide[owners], precision=lax.Precision.HIGHEST)
        product = product * live_part[:, None, None]
        return (carry, jax.ops.segment_sum(product, tile_ids, num_segments=TILES_PER_PLANE))
    unused, update = lax.scan(backward, jnp.zeros((), jnp.float32), stacked)
    update = update.reshape(NY // TILE, COLS // TILE, TILE, TILE, SLICES).transpose(0, 2, 1, 3, 4).reshape(NY, COLS, SLICES)
    volume = jnp.maximum(image + relax_step * update, 0.0)
    inside = jnp.ones((1, 1, 1), jnp.float32)
    for repeat in range(SWEEPS):
        volume = smooth_sweep(volume, inside)
    return (volume, residual)
```

```python
import functools

import jax
import jax.numpy as jnp
from jax import lax
from jax.experimental import pallas as pl
from jax.experimental.pallas import tpu as pltpu
from jax.sharding import PartitionSpec as P

TILE = 16
SWEEPS = 4
EDGE = 8
GROUP = 8

smooth_square = 0.09
flow_step = 0.04
relax_step = 4.0

SMEM = pl.BlockSpec(memory_space=pltpu.SMEM)
VMEM = pl.BlockSpec(memory_space=pltpu.VMEM)
ANY = pl.BlockSpec(memory_space=pl.ANY)
PARAMS = pltpu.CompilerParams(vmem_limit_bytes=48 * 1024 * 1024)


def relative_block(bits, position):
    block = 0
    for stage, bit in enumerate(bits):
        block |= ((position >> (len(bits) - 1 - stage)) & 1) << bit
    return block


def weight_copies(weights, held, sems):
    slots = held.shape[0]
    return [
        pltpu.make_async_copy(
            weights.at[pl.ds(first, GROUP)], held.at[pl.ds(first, GROUP)], sems.at[first // GROUP]
        )
        for first in range(0, slots, GROUP)
    ]


def forward_kernel(
    orders, me, tile_ids, blocks, owner, count, image, weights,
    a_keep, a_send, b_keep, b_send, pixels, held, turned, total, image_sem, sems,
):
    slots, voxels, rays = held.shape
    parts = total.shape[0] - 1
    half = rays // 2
    image_copy = pltpu.make_async_copy(image, pixels, image_sem)
    image_copy.start()
    for copy in weight_copies(weights, held, sems):
        copy.start()
    total[...] = jnp.zeros_like(total)
    image_copy.wait()
    for t in range(turned.shape[0]):
        tile = pixels[:, t * TILE : (t + 1) * TILE, :].reshape(voxels, pixels.shape[2])
        turned[t] = tile.T.astype(jnp.bfloat16)

    def step(group, carry):
        first = pl.multiple_of(group * GROUP, GROUP)
        pltpu.make_async_copy(
            weights.at[pl.ds(first, GROUP)], held.at[pl.ds(first, GROUP)], sems.at[group]
        ).wait()
        for k in range(GROUP):
            s = first + k
            to = jnp.where(s < count[0], owner[blocks[s]] ^ me[0], parts)
            total[to] += jnp.dot(
                turned[tile_ids[s]], held[s], preferred_element_type=jnp.float32
            )
        return carry

    lax.fori_loop(0, slots // GROUP, step, 0)
    for keep, send, order, low in ((a_keep, a_send, orders[0], 0), (b_keep, b_send, orders[1], half)):
        for p in range(parts // 2):
            keep[p] = total[relative_block(order, p), :, low : low + half]
            send[p] = total[relative_block(order, p + parts // 2), :, low : low + half].astype(jnp.bfloat16)


def residual_kernel(low, keep, got, measured, residual):
    half = residual.shape[1]
    projection = (keep[0] + got[0].astype(jnp.float32)).T
    mismatch = measured[0, low : low + half, :] - projection
    residual[0] = (mismatch / jnp.sqrt(1.0 + mismatch * mismatch)).astype(jnp.bfloat16)


def backward_kernel(
    orders, me, cut, tile_ids, blocks, owner, count, a_low, a_high, b_low, b_high, image, weights,
    relaxed, first_rows, last_rows, strip, pixels, held, spread, total, image_sem, sems,
):
    slots, voxels, rays = held.shape
    parts = spread.shape[0]
    tiles = total.shape[0] - 1
    half = rays // 2
    rows, cols, slices = relaxed.shape
    image_copy = pltpu.make_async_copy(image, pixels, image_sem)
    image_copy.start()
    for copy in weight_copies(weights, held, sems):
        copy.start()
    total[...] = jnp.zeros_like(total)
    for p in range(parts // 2):
        spread[relative_block(orders[0], p), :half] = a_low[p]
        spread[relative_block(orders[0], p + parts // 2), :half] = a_high[p]
        spread[relative_block(orders[1], p), half:] = b_low[p]
        spread[relative_block(orders[1], p + parts // 2), half:] = b_high[p]

    def step(group, carry):
        first = pl.multiple_of(group * GROUP, GROUP)
        pltpu.make_async_copy(
            weights.at[pl.ds(first, GROUP)], held.at[pl.ds(first, GROUP)], sems.at[group]
        ).wait()
        for k in range(GROUP):
            s = first + k
            to = jnp.where(s < count[0], tile_ids[s], tiles)
            total[to] += jnp.dot(
                held[s], spread[owner[blocks[s]] ^ me[0]], preferred_element_type=jnp.float32
            )
        return carry

    lax.fori_loop(0, slots // GROUP, step, 0)
    image_copy.wait()
    for t in range(tiles):
        span = slice(t * TILE, (t + 1) * TILE)
        update = total[t].reshape(rows, TILE, slices)
        relaxed[:, span, :] = jnp.maximum(pixels[:, span, :] + relax_step * update, 0.0)
    for i in range(SWEEPS):
        first_rows[i * cols : (i + 1) * cols] = relaxed[i].astype(jnp.bfloat16)
        last_rows[i * cols : (i + 1) * cols] = relaxed[rows - SWEEPS + i].astype(jnp.bfloat16)
    lane = lax.broadcasted_iota(jnp.int32, (cols, slices), 1)
    start = jnp.where(cut[0] == 0, slices - EDGE, 0)
    edges = jnp.zeros((cols, slices), jnp.float32)
    for i in range(rows):
        moved = pltpu.roll(relaxed[i], (i * EDGE - start + slices) % slices, 1)
        edges = jnp.where(lane // EDGE == i, moved, edges)
    strip[...] = edges.T.reshape(rows, EDGE, cols)


def shifted(x, axis, by):
    size = x.shape[axis]
    place = lax.broadcasted_iota(jnp.int32, x.shape, axis)
    if by > 0:
        return jnp.where(place == 0, 0.0, pltpu.roll(x, 1, axis))
    return jnp.where(place == size - 1, 0.0, pltpu.roll(x, size - 1, axis))


def flows(cell, below):
    rise_rows = below - cell
    rise_inner = shifted(cell, 0, -1) - cell
    rise_outer = shifted(cell, 1, -1) - cell
    scale = lax.rsqrt(
        smooth_square + rise_rows * rise_rows + rise_inner * rise_inner + rise_outer * rise_outer
    )
    return rise_rows * scale, rise_inner * scale, rise_outer * scale


def sweeps_over(field, rows, has_low, has_high):
    for sweep in range(1, SWEEPS + 1):

        @pl.when(has_low == 0)
        def _():
            field[SWEEPS - 1] = field[SWEEPS]

        @pl.when(has_high == 0)
        def _():
            field[SWEEPS + rows] = jnp.zeros(field.shape[1:], field.dtype)

        def body(i, before):
            cell = field[i]
            flow_rows, flow_inner, flow_outer = flows(cell, field[i + 1])
            diverge = flow_rows - before
            diverge = diverge + (flow_inner - shifted(flow_inner, 0, 1))
            diverge = diverge + (flow_outer - shifted(flow_outer, 1, 1))
            field[i] = cell + flow_step * diverge
            return flow_rows

        before = flows(field[sweep - 1], field[sweep])[0]
        lax.fori_loop(sweep, rows + 2 * SWEEPS - sweep, body, before)


def sweep_kernel(me, cut, relaxed, strip, from_low, from_high, volume, field, narrow, *, planes):
    rows, cols, slices = relaxed.shape
    body = SWEEPS * cols
    field[SWEEPS : SWEEPS + rows] = relaxed[...]
    narrow[SWEEPS : SWEEPS + rows] = strip[...]
    for start, halo in ((0, from_low), (SWEEPS + rows, from_high)):
        field[start : start + SWEEPS] = halo[:body].astype(jnp.float32).reshape(SWEEPS, cols, slices)
        narrow[start : start + SWEEPS] = (
            halo[body:].astype(jnp.float32).reshape(SWEEPS, 2 * EDGE, cols)
        )
    has_low = (me[0] > 0).astype(jnp.int32)
    has_high = (me[0] < planes - 1).astype(jnp.int32)
    sweeps_over(narrow, rows, has_low, has_high)
    sweeps_over(field, rows, has_low, has_high)
    low_side = cut[0] == 0
    mine = narrow[SWEEPS : SWEEPS + rows]
    mine = jnp.where(low_side, mine[:, :EDGE], mine[:, EDGE:])
    turned = mine.reshape(rows * EDGE, cols).T
    lane = lax.broadcasted_iota(jnp.int32, (cols, slices), 1)
    start = jnp.where(low_side, slices - EDGE, 0)
    first = jnp.where(low_side, slices - SWEEPS, 0)
    patch = (lane >= first) & (lane < first + SWEEPS)
    for i in range(rows):
        moved = pltpu.roll(turned, (start - i * EDGE + slices) % slices, 1)
        volume[i] = jnp.where(patch, moved, field[SWEEPS + i])


def sum_chain(keep, send, order, planes):
    for stage, bit in enumerate(order):
        got = lax.ppermute(send, "plane", [(i, i ^ (1 << bit)) for i in range(planes)])
        if stage == len(order) - 1:
            return keep, got
        total = keep + got.astype(jnp.float32)
        left = total.shape[0] // 2
        keep, send = total[:left], total[left:].astype(jnp.bfloat16)


def spread_chain(piece, order, planes):
    for stage, bit in reversed(list(enumerate(order))):
        got = lax.ppermute(piece, "plane", [(i, i ^ (1 << bit)) for i in range(planes)])
        if stage == 0:
            return piece, got
        piece = jnp.concatenate([piece, got], axis=0)


def per_device(
    image,
    projection_weight_tiles,
    pair_tile_index,
    pair_ray_block,
    ray_owner,
    active_pair_count,
    measured,
):
    rows, cols, slices = image.shape
    slots, voxels, rays = projection_weight_tiles.shape
    tiles = (rows // TILE) * (cols // TILE)
    planes = lax.axis_size("plane")
    parts = ray_owner.shape[0]
    half = rays // 2
    bits = planes.bit_length() - 1
    plain = tuple(range(bits))
    swapped = (1, 0) + plain[2:]
    orders = (plain, swapped)
    me = lax.axis_index("plane").astype(jnp.int32).reshape(1)
    cut = lax.axis_index("cuts").astype(jnp.int32).reshape(1)
    shape = jax.ShapeDtypeStruct
    f32, bf16 = jnp.float32, jnp.bfloat16

    kept, sent = shape((parts // 2, slices, half), f32), shape((parts // 2, slices, half), bf16)
    a_keep, a_send, b_keep, b_send = pl.pallas_call(
        functools.partial(forward_kernel, orders),
        out_shape=(kept, sent, kept, sent),
        in_specs=[SMEM] * 5 + [ANY, ANY],
        out_specs=(VMEM,) * 4,
        scratch_shapes=[
            pltpu.VMEM((rows, cols, slices), f32),
            pltpu.VMEM((slots, voxels, rays), bf16),
            pltpu.VMEM((tiles, slices, voxels), bf16),
            pltpu.VMEM((parts + 1, slices, rays), f32),
            pltpu.SemaphoreType.DMA,
            pltpu.SemaphoreType.DMA((slots // GROUP,)),
        ],
        compiler_params=PARAMS,
        name="forward",
    )(me, pair_tile_index, pair_ray_block, ray_owner, active_pair_count, image, projection_weight_tiles)

    pieces = []
    for low, keep, send, order in ((0, a_keep, a_send, plain), (half, b_keep, b_send, swapped)):
        keep, got = sum_chain(keep, send, order, planes)
        pieces.append(
            pl.pallas_call(
                functools.partial(residual_kernel, low),
                out_shape=shape((1, half, slices), bf16),
                in_specs=[VMEM] * 3,
                out_specs=VMEM,
                name="residual",
            )(keep, got, measured)
        )
    residual = jnp.concatenate(pieces, axis=1)
    a_low, a_high = spread_chain(pieces[0], plain, planes)
    b_low, b_high = spread_chain(pieces[1], swapped, planes)

    relaxed, first_rows, last_rows, strip = pl.pallas_call(
        functools.partial(backward_kernel, orders),
        out_shape=(
            shape((rows, cols, slices), f32),
            shape((SWEEPS * cols, slices), bf16),
            shape((SWEEPS * cols, slices), bf16),
            shape((rows, EDGE, cols), f32),
        ),
        in_specs=[SMEM] * 6 + [VMEM] * 4 + [ANY, ANY],
        out_specs=(VMEM,) * 4,
        scratch_shapes=[
            pltpu.VMEM((rows, cols, slices), f32),
            pltpu.VMEM((slots, voxels, rays), bf16),
            pltpu.VMEM((parts, rays, slices), bf16),
            pltpu.VMEM((tiles + 1, voxels, slices), f32),
            pltpu.SemaphoreType.DMA,
            pltpu.SemaphoreType.DMA((slots // GROUP,)),
        ],
        compiler_params=PARAMS,
        name="backward",
    )(
        me, cut, pair_tile_index, pair_ray_block, ray_owner, active_pair_count,
        a_low, a_high, b_low, b_high, image, projection_weight_tiles,
    )

    other = lax.ppermute(strip, "cuts", [(0, 1), (1, 0)])
    both = jnp.where(
        cut[0] == 0, jnp.concatenate([strip, other], 1), jnp.concatenate([other, strip], 1)
    )

    def with_strip(main, part):
        return jnp.concatenate([main, part.astype(bf16).reshape(-1, cols)], axis=0)

    upward = [(i, i + 1) for i in range(planes - 1)]
    downward = [(i + 1, i) for i in range(planes - 1)]
    from_low = lax.ppermute(with_strip(last_rows, both[rows - SWEEPS :]), "plane", upward)
    from_high = lax.ppermute(with_strip(first_rows, both[:SWEEPS]), "plane", downward)

    volume = pl.pallas_call(
        functools.partial(sweep_kernel, planes=planes),
        out_shape=shape((rows, cols, slices), f32),
        in_specs=[SMEM, SMEM] + [VMEM] * 4,
        out_specs=VMEM,
        scratch_shapes=[
            pltpu.VMEM((rows + 2 * SWEEPS, cols, slices), f32),
            pltpu.VMEM((rows + 2 * SWEEPS, 2 * EDGE, cols), f32),
        ],
        compiler_params=PARAMS,
        name="sweeps",
    )(me, cut, relaxed, both, from_low, from_high)
    return (volume, residual)


def solution(mesh):
    placed = (
        P("plane", None, "cuts"),
        P("plane", None, None),
        P("plane"),
        P("plane"),
        P(),
        P("plane"),
        P("plane", None, "cuts"),
    )
    return jax.shard_map(
        per_device,
        mesh=mesh,
        in_specs=placed,
        out_specs=(P("plane", None, "cuts"), P("plane", None, "cuts")),
        check_vma=False,
    )
```

```python
import functools

import jax
import jax.numpy as jnp
from jax import lax
from jax.experimental import pallas as pl
from jax.experimental.pallas import tpu as pltpu
from jax.sharding import PartitionSpec as P

TILE = 16
SWEEPS = 4
EDGE = 8
GROUP = 8

smooth_square = 0.09
flow_step = 0.04
relax_step = 4.0

VMEM = pl.BlockSpec(memory_space=pltpu.VMEM)
HBM = pl.BlockSpec(memory_space=pltpu.HBM)
PARAMS = pltpu.CompilerParams(vmem_limit_bytes=48 * 1024 * 1024)


def relative_block(bits, position):
    block = 0
    for stage, bit in enumerate(bits):
        block |= ((position >> (len(bits) - 1 - stage)) & 1) << bit
    return block


def weight_copies(weights, held, sems):
    slots = held.shape[0]
    return [
        pltpu.make_async_copy(
            weights.at[pl.ds(first, GROUP)], held.at[pl.ds(first, GROUP)], sems.at[first // GROUP]
        )
        for first in range(0, slots, GROUP)
    ]


def list_copies(lists, scalars):
    held, sem = scalars[:-1], scalars[-1]
    copies = [pltpu.make_async_copy(a, b, sem.at[i]) for i, (a, b) in enumerate(zip(lists, held))]
    for copy in copies:
        copy.start()
    return copies, held


def forward_kernel(
    orders, tile_ids, blocks, owner, count, image, weights,
    a_keep, a_send, b_keep, b_send, pixels, held, turned, total, image_sem, sems, *scalars,
):
    me = lax.axis_index("plane")
    lists, (tile_ids, blocks, owner, count) = list_copies((tile_ids, blocks, owner, count), scalars)
    slots, voxels, rays = held.shape
    parts = total.shape[0] - 1
    half = rays // 2
    image_copy = pltpu.make_async_copy(image, pixels, image_sem)
    image_copy.start()
    for copy in weight_copies(weights, held, sems):
        copy.start()
    total[...] = jnp.zeros_like(total)
    image_copy.wait()
    for t in range(turned.shape[0]):
        tile = pixels[:, t * TILE : (t + 1) * TILE, :].reshape(voxels, pixels.shape[2])
        turned[t] = tile.T.astype(jnp.bfloat16)

    for copy in lists:
        copy.wait()

    def step(group, carry):
        first = pl.multiple_of(group * GROUP, GROUP)
        pltpu.make_async_copy(
            weights.at[pl.ds(first, GROUP)], held.at[pl.ds(first, GROUP)], sems.at[group]
        ).wait()
        for k in range(GROUP):
            s = first + k
            to = jnp.where(s < count[0], owner[blocks[s]] ^ me, parts)
            total[to] += jnp.dot(
                turned[tile_ids[s]], held[s], preferred_element_type=jnp.float32
            )
        return carry

    lax.fori_loop(0, slots // GROUP, step, 0)
    for keep, send, order, low in ((a_keep, a_send, orders[0], 0), (b_keep, b_send, orders[1], half)):
        for p in range(parts // 2):
            keep[p] = total[relative_block(order, p), :, low : low + half]
            send[p] = total[relative_block(order, p + parts // 2), :, low : low + half].astype(jnp.bfloat16)


def residual_kernel(low, keep, got, measured, residual):
    half = residual.shape[1]
    projection = (keep[0] + got[0].astype(jnp.float32)).T
    mismatch = measured[0, low : low + half, :] - projection
    residual[0] = (mismatch / jnp.sqrt(1.0 + mismatch * mismatch)).astype(jnp.bfloat16)


def backward_kernel(
    orders, tile_ids, blocks, owner, count, a_low, a_high, b_low, b_high, image, weights,
    relaxed, first_rows, last_rows, strip, pixels, held, spread, total, image_sem, sems, *scalars,
):
    me = lax.axis_index("plane")
    cut = lax.axis_index("cuts")
    lists, (tile_ids, blocks, owner, count) = list_copies((tile_ids, blocks, owner, count), scalars)
    slots, voxels, rays = held.shape
    parts = spread.shape[0]
    tiles = total.shape[0] - 1
    half = rays // 2
    rows, cols, slices = relaxed.shape
    image_copy = pltpu.make_async_copy(image, pixels, image_sem)
    image_copy.start()
    for copy in weight_copies(weights, held, sems):
        copy.start()
    total[...] = jnp.zeros_like(total)
    for p in range(parts // 2):
        spread[relative_block(orders[0], p), :half] = a_low[p]
        spread[relative_block(orders[0], p + parts // 2), :half] = a_high[p]
        spread[relative_block(orders[1], p), half:] = b_low[p]
        spread[relative_block(orders[1], p + parts // 2), half:] = b_high[p]

    for copy in lists:
        copy.wait()

    def step(group, carry):
        first = pl.multiple_of(group * GROUP, GROUP)
        pltpu.make_async_copy(
            weights.at[pl.ds(first, GROUP)], held.at[pl.ds(first, GROUP)], sems.at[group]
        ).wait()
        for k in range(GROUP):
            s = first + k
            to = jnp.where(s < count[0], tile_ids[s], tiles)
            total[to] += jnp.dot(
                held[s], spread[owner[blocks[s]] ^ me], preferred_element_type=jnp.float32
            )
        return carry

    lax.fori_loop(0, slots // GROUP, step, 0)
    image_copy.wait()
    for t in range(tiles):
        span = slice(t * TILE, (t + 1) * TILE)
        update = total[t].reshape(rows, TILE, slices)
        relaxed[:, span, :] = jnp.maximum(pixels[:, span, :] + relax_step * update, 0.0)
    for i in range(SWEEPS):
        first_rows[i * cols : (i + 1) * cols] = relaxed[i].astype(jnp.bfloat16)
        last_rows[i * cols : (i + 1) * cols] = relaxed[rows - SWEEPS + i].astype(jnp.bfloat16)
    lane = lax.broadcasted_iota(jnp.int32, (cols, slices), 1)
    start = jnp.where(cut == 0, slices - EDGE, 0)
    edges = jnp.zeros((cols, slices), jnp.float32)
    for i in range(rows):
        moved = pltpu.roll(relaxed[i], (i * EDGE - start + slices) % slices, 1)
        edges = jnp.where(lane // EDGE == i, moved, edges)
    strip[...] = edges.T.reshape(rows, EDGE, cols)


def shifted(x, axis, by):
    size = x.shape[axis]
    place = lax.broadcasted_iota(jnp.int32, x.shape, axis)
    if by > 0:
        return jnp.where(place == 0, 0.0, pltpu.roll(x, 1, axis))
    return jnp.where(place == size - 1, 0.0, pltpu.roll(x, size - 1, axis))


def flows(cell, below):
    rise_rows = below - cell
    rise_inner = shifted(cell, 0, -1) - cell
    rise_outer = shifted(cell, 1, -1) - cell
    scale = lax.rsqrt(
        smooth_square + rise_rows * rise_rows + rise_inner * rise_inner + rise_outer * rise_outer
    )
    return rise_rows * scale, rise_inner * scale, rise_outer * scale


def sweeps_over(fields, rows, has_low, has_high):
    def advance(field, i, before):
        cell = field[i]
        flow_rows, flow_inner, flow_outer = flows(cell, field[i + 1])
        diverge = flow_rows - before
        diverge = diverge + (flow_inner - shifted(flow_inner, 0, 1))
        diverge = diverge + (flow_outer - shifted(flow_outer, 1, 1))
        field[i] = cell + flow_step * diverge
        return flow_rows

    for sweep in range(1, SWEEPS + 1):

        @pl.when(has_low == 0)
        def _():
            for field in fields:
                field[SWEEPS - 1] = field[SWEEPS]

        @pl.when(has_high == 0)
        def _():
            for field in fields:
                field[SWEEPS + rows] = jnp.zeros(field.shape[1:], field.dtype)

        def body(i, before):
            return tuple(advance(field, i, flow) for field, flow in zip(fields, before))

        before = tuple(flows(field[sweep - 1], field[sweep])[0] for field in fields)
        lax.fori_loop(sweep, rows + 2 * SWEEPS - sweep, body, before, unroll=3)


def sweep_kernel(relaxed, strip, from_low, from_high, volume, field, narrow, *, planes):
    rows, cols, slices = relaxed.shape
    me, cut = lax.axis_index("plane"), lax.axis_index("cuts")
    body = SWEEPS * cols
    field[SWEEPS : SWEEPS + rows] = relaxed[...]
    narrow[SWEEPS : SWEEPS + rows] = strip[...]
    for start, halo in ((0, from_low), (SWEEPS + rows, from_high)):
        field[start : start + SWEEPS] = halo[:body].astype(jnp.float32).reshape(SWEEPS, cols, slices)
        narrow[start : start + SWEEPS] = (
            halo[body:].astype(jnp.float32).reshape(SWEEPS, 2 * EDGE, cols)
        )
    has_low = (me > 0).astype(jnp.int32)
    has_high = (me < planes - 1).astype(jnp.int32)
    sweeps_over((field, narrow), rows, has_low, has_high)
    low_side = cut == 0
    mine = narrow[SWEEPS : SWEEPS + rows]
    mine = jnp.where(low_side, mine[:, :EDGE], mine[:, EDGE:])
    turned = mine.reshape(rows * EDGE, cols).T
    lane = lax.broadcasted_iota(jnp.int32, (cols, slices), 1)
    start = jnp.where(low_side, slices - EDGE, 0)
    first = jnp.where(low_side, slices - SWEEPS, 0)
    patch = (lane >= first) & (lane < first + SWEEPS)
    for i in range(rows):
        moved = pltpu.roll(turned, (start - i * EDGE + slices) % slices, 1)
        volume[i] = jnp.where(patch, moved, field[SWEEPS + i])


def sum_chain(keep, send, order, planes):
    for stage, bit in enumerate(order):
        got = lax.ppermute(send, "plane", [(i, i ^ (1 << bit)) for i in range(planes)])
        if stage == len(order) - 1:
            return keep, got
        total = keep + got.astype(jnp.float32)
        left = total.shape[0] // 2
        keep, send = total[:left], total[left:].astype(jnp.bfloat16)


def spread_chain(piece, order, planes):
    for stage, bit in reversed(list(enumerate(order))):
        got = lax.ppermute(piece, "plane", [(i, i ^ (1 << bit)) for i in range(planes)])
        if stage == 0:
            return piece, got
        piece = jnp.concatenate([piece, got], axis=0)


def per_device(
    image,
    projection_weight_tiles,
    pair_tile_index,
    pair_ray_block,
    ray_owner,
    active_pair_count,
    measured,
):
    rows, cols, slices = image.shape
    slots, voxels, rays = projection_weight_tiles.shape
    tiles = (rows // TILE) * (cols // TILE)
    planes = lax.axis_size("plane")
    parts = ray_owner.shape[0]
    half = rays // 2
    bits = planes.bit_length() - 1
    plain = tuple(range(bits))
    swapped = (1, 0) + plain[2:]
    orders = (plain, swapped)
    cut = lax.axis_index("cuts")
    shape = jax.ShapeDtypeStruct
    f32, bf16 = jnp.float32, jnp.bfloat16

    scalars = [
        *(pltpu.SMEM(a.shape, jnp.int32) for a in (pair_tile_index, pair_ray_block, ray_owner, active_pair_count)),
        pltpu.SemaphoreType.DMA((4,)),
    ]

    kept, sent = shape((parts // 2, slices, half), f32), shape((parts // 2, slices, half), bf16)
    a_keep, a_send, b_keep, b_send = pl.pallas_call(
        functools.partial(forward_kernel, orders),
        out_shape=(kept, sent, kept, sent),
        in_specs=[HBM] * 6,
        out_specs=(VMEM,) * 4,
        scratch_shapes=[
            pltpu.VMEM((rows, cols, slices), f32),
            pltpu.VMEM((slots, voxels, rays), bf16),
            pltpu.VMEM((tiles, slices, voxels), bf16),
            pltpu.VMEM((parts + 1, slices, rays), f32),
            pltpu.SemaphoreType.DMA,
            pltpu.SemaphoreType.DMA((slots // GROUP,)),
            *scalars,
        ],
        compiler_params=PARAMS,
        name="forward",
    )(pair_tile_index, pair_ray_block, ray_owner, active_pair_count, image, projection_weight_tiles)

    pieces = []
    for low, keep, send, order in ((0, a_keep, a_send, plain), (half, b_keep, b_send, swapped)):
        keep, got = sum_chain(keep, send, order, planes)
        pieces.append(
            pl.pallas_call(
                functools.partial(residual_kernel, low),
                out_shape=shape((1, half, slices), bf16),
                in_specs=[VMEM] * 3,
                out_specs=VMEM,
                compiler_params=PARAMS,
                name="residual",
            )(keep, got, measured)
        )
    residual = jnp.concatenate(pieces, axis=1)
    a_low, a_high = spread_chain(pieces[0], plain, planes)
    b_low, b_high = spread_chain(pieces[1], swapped, planes)

    relaxed, first_rows, last_rows, strip = pl.pallas_call(
        functools.partial(backward_kernel, orders),
        out_shape=(
            shape((rows, cols, slices), f32),
            shape((SWEEPS * cols, slices), bf16),
            shape((SWEEPS * cols, slices), bf16),
            shape((rows, EDGE, cols), f32),
        ),
        in_specs=[HBM] * 4 + [VMEM] * 4 + [HBM, HBM],
        out_specs=(VMEM,) * 4,
        scratch_shapes=[
            pltpu.VMEM((rows, cols, slices), f32),
            pltpu.VMEM((slots, voxels, rays), bf16),
            pltpu.VMEM((parts, rays, slices), bf16),
            pltpu.VMEM((tiles + 1, voxels, slices), f32),
            pltpu.SemaphoreType.DMA,
            pltpu.SemaphoreType.DMA((slots // GROUP,)),
            *scalars,
        ],
        compiler_params=PARAMS,
        name="backward",
    )(
        pair_tile_index, pair_ray_block, ray_owner, active_pair_count,
        a_low, a_high, b_low, b_high, image, projection_weight_tiles,
    )

    other = lax.ppermute(strip, "cuts", [(0, 1), (1, 0)])
    both = jnp.where(
        cut == 0, jnp.concatenate([strip, other], 1), jnp.concatenate([other, strip], 1)
    )

    def with_strip(main, part):
        return jnp.concatenate([main, part.astype(bf16).reshape(-1, cols)], axis=0)

    upward = [(i, i + 1) for i in range(planes - 1)]
    downward = [(i + 1, i) for i in range(planes - 1)]
    from_low = lax.ppermute(with_strip(last_rows, both[rows - SWEEPS :]), "plane", upward)
    from_high = lax.ppermute(with_strip(first_rows, both[:SWEEPS]), "plane", downward)

    volume = pl.pallas_call(
        functools.partial(sweep_kernel, planes=planes),
        out_shape=shape((rows, cols, slices), f32),
        in_specs=[VMEM] * 4,
        out_specs=VMEM,
        scratch_shapes=[
            pltpu.VMEM((rows + 2 * SWEEPS, cols, slices), f32),
            pltpu.VMEM((rows + 2 * SWEEPS, 2 * EDGE, cols), f32),
        ],
        compiler_params=PARAMS,
        name="sweeps",
    )(relaxed, both, from_low, from_high)
    return (volume, residual)


def solution(mesh):
    placed = (
        P("plane", None, "cuts"),
        P("plane", None, None),
        P("plane"),
        P("plane"),
        P(),
        P("plane"),
        P("plane", None, "cuts"),
    )
    return jax.shard_map(
        per_device,
        mesh=mesh,
        in_specs=placed,
        out_specs=(P("plane", None, "cuts"), P("plane", None, "cuts")),
        check_vma=False,
    )
```

```python
import functools

import jax
import jax.numpy as jnp
from jax import lax
from jax.experimental import pallas as pl
from jax.experimental.pallas import tpu as pltpu
from jax.sharding import PartitionSpec as P

TILE = 16
SWEEPS = 4
EDGE = 8
GROUP = 16
BACK_GROUP = 32

smooth_square = 0.09
flow_step = 0.04
relax_step = 4.0

VMEM = pl.BlockSpec(memory_space=pltpu.VMEM)
HBM = pl.BlockSpec(memory_space=pltpu.HBM)
PARAMS = pltpu.CompilerParams(vmem_limit_bytes=24 * 1024 * 1024)


def relative_block(bits, position):
    block = 0
    for stage, bit in enumerate(bits):
        block |= ((position >> (len(bits) - 1 - stage)) & 1) << bit
    return block


def weight_copy(weights, held, sems, group):
    span = pl.ds(group * GROUP, GROUP)
    return pltpu.make_async_copy(weights.at[span], held.at[span], sems.at[group])


def list_copies(lists, scalars):
    held, sem = scalars[:-1], scalars[-1]
    copies = [pltpu.make_async_copy(a, b, sem.at[i]) for i, (a, b) in enumerate(zip(lists, held))]
    for copy in copies:
        copy.start()
    return copies, held


def forward_kernel(
    orders, tile_ids, blocks, owner, count, image, weights,
    a_keep, a_send, b_keep, b_send, held, pixels, turned, total, image_sem, sems, *scalars,
):
    me = lax.axis_index("plane")
    lists, (tile_ids, blocks, owner, count) = list_copies((tile_ids, blocks, owner, count), scalars)
    slots, voxels, rays = held.shape
    parts = total.shape[0] - 1
    half = rays // 2
    image_copy = pltpu.make_async_copy(image, pixels, image_sem)
    image_copy.start()
    for group in range(slots // GROUP):
        weight_copy(weights, held, sems, group).start()
    total[...] = jnp.zeros_like(total)
    image_copy.wait()
    for t in range(turned.shape[0]):
        tile = pixels[:, t * TILE : (t + 1) * TILE, :].reshape(voxels, pixels.shape[2])
        turned[t] = tile.T.astype(jnp.bfloat16)

    for copy in lists:
        copy.wait()

    def step(group, carry):
        weight_copy(weights, held, sems, group).wait()
        for k in range(GROUP):
            s = group * GROUP + k
            to = jnp.where(s < count[0], owner[blocks[s]] ^ me, parts)
            total[to] += jnp.dot(
                turned[tile_ids[s]], held[s], preferred_element_type=jnp.float32
            )
        return carry

    lax.fori_loop(0, slots // GROUP, step, 0)
    for keep, send, order, low in ((a_keep, a_send, orders[0], 0), (b_keep, b_send, orders[1], half)):
        for p in range(parts // 2):
            keep[p] = total[relative_block(order, p), :, low : low + half]
            send[p] = total[relative_block(order, p + parts // 2), :, low : low + half].astype(jnp.bfloat16)


def residual_kernel(low, keep, got, measured, residual):
    half = residual.shape[1]
    projection = (keep[0] + got[0].astype(jnp.float32)).T
    mismatch = measured[0, low : low + half, :] - projection
    residual[0] = (mismatch / jnp.sqrt(1.0 + mismatch * mismatch)).astype(jnp.bfloat16)


def backward_kernel(
    orders, tile_ids, blocks, owner, count, a_low, a_high, b_low, b_high, image, weights,
    relaxed, to_near, to_far, strip, spread, total, *scalars,
):
    me = lax.axis_index("plane")
    cut = lax.axis_index("cuts")
    lists, (tile_ids, blocks, owner, count) = list_copies((tile_ids, blocks, owner, count), scalars)
    slots, voxels, rays = weights.shape
    parts = spread.shape[0]
    tiles = total.shape[0] - 1
    half = rays // 2
    rows, cols, slices = relaxed.shape
    total[...] = jnp.zeros_like(total)
    for p in range(parts // 2):
        spread[relative_block(orders[0], p), :half] = a_low[p]
        spread[relative_block(orders[0], p + parts // 2), :half] = a_high[p]
        spread[relative_block(orders[1], p), half:] = b_low[p]
        spread[relative_block(orders[1], p + parts // 2), half:] = b_high[p]

    for copy in lists:
        copy.wait()

    def step(group, carry):
        for k in range(BACK_GROUP):
            s = group * BACK_GROUP + k
            to = jnp.where(s < count[0], tile_ids[s], tiles)
            total[to] += jnp.dot(
                weights[s], spread[owner[blocks[s]] ^ me], preferred_element_type=jnp.float32
            )
        return carry

    lax.fori_loop(0, slots // BACK_GROUP, step, 0)
    for t in range(tiles):
        span = slice(t * TILE, (t + 1) * TILE)
        update = total[t].reshape(rows, TILE, slices)
        relaxed[:, span, :] = jnp.maximum(image[:, span, :] + relax_step * update, 0.0)
    even = lax.rem(me, 2) == 0
    for side, start in (
        (to_near, jnp.where(even, rows - SWEEPS, 0)),
        (to_far, jnp.where(even, 0, rows - SWEEPS)),
    ):
        for i in range(SWEEPS):
            side[i * cols : (i + 1) * cols] = relaxed[start + i].astype(jnp.bfloat16)
    lane = lax.broadcasted_iota(jnp.int32, (cols, slices), 1)
    start = jnp.where(cut == 0, slices - EDGE, 0)
    edges = jnp.zeros((cols, slices), jnp.float32)
    for i in range(rows):
        moved = pltpu.roll(relaxed[i], (i * EDGE - start + slices) % slices, 1)
        edges = jnp.where(lane // EDGE == i, moved, edges)
    strip[...] = edges.T.reshape(rows, EDGE, cols)


def shifted(x, axis, by):
    size = x.shape[axis]
    place = lax.broadcasted_iota(jnp.int32, x.shape, axis)
    if by > 0:
        return jnp.where(place == 0, 0.0, pltpu.roll(x, 1, axis))
    return jnp.where(place == size - 1, 0.0, pltpu.roll(x, size - 1, axis))


def flows(cell, below):
    rise_rows = below - cell
    rise_inner = shifted(cell, 0, -1) - cell
    rise_outer = shifted(cell, 1, -1) - cell
    scale = lax.rsqrt(
        smooth_square + rise_rows * rise_rows + rise_inner * rise_inner + rise_outer * rise_outer
    )
    return rise_rows * scale, rise_inner * scale, rise_outer * scale


def advance(cell, below, before):
    flow_rows, flow_inner, flow_outer = flows(cell, below)
    diverge = flow_rows - before
    diverge = diverge + (flow_inner - shifted(flow_inner, 0, 1))
    diverge = diverge + (flow_outer - shifted(flow_outer, 1, 1))
    return cell + flow_step * diverge, flow_rows


def inner_kernel(relaxed, strip, *refs):
    rows = relaxed.shape[0]
    fields, results, saves = refs[4:6], refs[0:2], refs[2:4]
    for field, start in zip(fields, (relaxed, strip)):
        field[...] = start[...]
    for k in range(SWEEPS):
        for field, save in zip(fields, saves):
            save[k, 0:2] = field[k : k + 2]
            save[k, 2:4] = field[rows - 2 - k : rows - k]

        def body(i, before):
            after = []
            for field, flow in zip(fields, before):
                field[i], flow = advance(field[i], field[i + 1], flow)
                after.append(flow)
            return tuple(after)

        before = tuple(flows(field[k], field[k + 1])[0] for field in fields)
        lax.fori_loop(k + 1, rows - 1 - k, body, before, unroll=3)
    for field, result in zip(fields, results):
        result[...] = field[SWEEPS : rows - SWEEPS]


def edge_kernel(
    inner, inner_strip, saved, saved_strip, from_near, from_far, volume,
    low_field, low_strip, high_field, high_strip, *, planes,
):
    rows, cols, slices = volume.shape
    me, cut = lax.axis_index("plane"), lax.axis_index("cuts")
    body_rows = SWEEPS * cols
    even = lax.rem(me, 2) == 0
    for other, this, field, strip, at in (
        (from_near, from_far, low_field, low_strip, (slice(0, 4),)),
        (from_far, from_near, high_field, high_strip, (0, slice(2, 6))),
    ):
        halo = jnp.where(even, this[...], other[...])
        field[at] = halo[:body_rows].astype(jnp.float32).reshape(SWEEPS, cols, slices)
        strip[at] = halo[body_rows:].astype(jnp.float32).reshape(SWEEPS, 2 * EDGE, cols)
    pairs = ((low_field, high_field, saved), (low_strip, high_strip, saved_strip))
    for k in range(SWEEPS):
        now, later = k % 2, (k + 1) % 2
        for low, high, save in pairs:
            low[4:6] = save[k, 0:2]
            high[now, 0:2] = save[k, 2:4]

        @pl.when(me == 0)
        def _():
            for low, _, _ in pairs:
                low[3 - k] = low[4 - k]

        @pl.when(me == planes - 1)
        def _():
            for _, high, _ in pairs:
                high[now, 2 + k] = jnp.zeros(high.shape[2:], high.dtype)

        def body(i, before):
            after = []
            for (low, high, _), (flow_low, flow_high) in zip(pairs, before):
                low[i - 1], flow_low = advance(low[i], low[i + 1], flow_low)
                high[later, i + 1], flow_high = advance(high[now, i], high[now, i + 1], flow_high)
                after.append((flow_low, flow_high))
            return tuple(after)

        before = tuple(
            (flows(low[0], low[1])[0], flows(high[now, 0], high[now, 1])[0]) for low, high, _ in pairs
        )
        lax.fori_loop(1, SWEEPS + 1, body, before, unroll=2)
    last = SWEEPS % 2
    low_side = cut == 0
    mine = jnp.concatenate([low_strip[0:4], inner_strip[...], high_strip[last, 2:6]], axis=0)
    mine = jnp.where(low_side, mine[:, :EDGE], mine[:, EDGE:])
    turned = mine.reshape(rows * EDGE, cols).T
    lane = lax.broadcasted_iota(jnp.int32, (cols, slices), 1)
    start = jnp.where(low_side, slices - EDGE, 0)
    first = jnp.where(low_side, slices - SWEEPS, 0)
    patch = (lane >= first) & (lane < first + SWEEPS)
    for i in range(rows):
        if i < SWEEPS:
            row = low_field[i]
        elif i < rows - SWEEPS:
            row = inner[i - SWEEPS]
        else:
            row = high_field[last, i - (rows - SWEEPS) + 2]
        moved = pltpu.roll(turned, (start - i * EDGE + slices) % slices, 1)
        volume[i] = jnp.where(patch, moved, row)


def sum_chain(keep, send, order, planes):
    for stage, bit in enumerate(order):
        got = lax.ppermute(send, "plane", [(i, i ^ (1 << bit)) for i in range(planes)])
        if stage == len(order) - 1:
            return keep, got
        total = keep + got.astype(jnp.float32)
        left = total.shape[0] // 2
        keep, send = total[:left], total[left:].astype(jnp.bfloat16)


def spread_chain(piece, order, planes):
    for stage, bit in reversed(list(enumerate(order))):
        got = lax.ppermute(piece, "plane", [(i, i ^ (1 << bit)) for i in range(planes)])
        if stage == 0:
            return piece, got
        piece = jnp.concatenate([piece, got], axis=0)


def per_device(
    image,
    projection_weight_tiles,
    pair_tile_index,
    pair_ray_block,
    ray_owner,
    active_pair_count,
    measured,
):
    rows, cols, slices = image.shape
    slots, voxels, rays = projection_weight_tiles.shape
    tiles = (rows // TILE) * (cols // TILE)
    planes = lax.axis_size("plane")
    parts = ray_owner.shape[0]
    half = rays // 2
    bits = planes.bit_length() - 1
    plain = tuple(range(bits))
    swapped = (1, 0) + plain[2:]
    orders = (plain, swapped)
    cut = lax.axis_index("cuts")
    shape = jax.ShapeDtypeStruct
    f32, bf16 = jnp.float32, jnp.bfloat16

    weights = pltpu.with_memory_space_constraint(projection_weight_tiles, pltpu.HBM)
    lists = [
        pltpu.with_memory_space_constraint(a, pltpu.HBM)
        for a in (pair_tile_index, pair_ray_block, ray_owner)
    ] + [active_pair_count]
    far_image = pltpu.with_memory_space_constraint(image, pltpu.HBM)
    scalars = [
        *(pltpu.SMEM(a.shape, jnp.int32) for a in (pair_tile_index, pair_ray_block, ray_owner, active_pair_count)),
        pltpu.SemaphoreType.DMA((4,)),
    ]

    kept, sent = shape((parts // 2, slices, half), f32), shape((parts // 2, slices, half), bf16)
    a_keep, a_send, b_keep, b_send, held = pl.pallas_call(
        functools.partial(forward_kernel, orders),
        out_shape=(kept, sent, kept, sent, shape(weights.shape, bf16)),
        in_specs=[HBM] * 6,
        out_specs=(VMEM,) * 5,
        scratch_shapes=[
            pltpu.VMEM((rows, cols, slices), f32),
            pltpu.VMEM((tiles, slices, voxels), bf16),
            pltpu.VMEM((parts + 1, slices, rays), f32),
            pltpu.SemaphoreType.DMA,
            pltpu.SemaphoreType.DMA((slots // GROUP,)),
            *scalars,
        ],
        compiler_params=PARAMS,
        name="forward",
    )(*lists, far_image, weights)

    pieces = []
    for low, keep, send, order in ((0, a_keep, a_send, plain), (half, b_keep, b_send, swapped)):
        keep, got = sum_chain(keep, send, order, planes)
        pieces.append(
            pl.pallas_call(
                functools.partial(residual_kernel, low),
                out_shape=shape((1, half, slices), bf16),
                in_specs=[VMEM] * 3,
                out_specs=VMEM,
                compiler_params=PARAMS,
                name="residual",
            )(keep, got, measured)
        )
    residual = jnp.concatenate(pieces, axis=1)
    a_low, a_high = spread_chain(pieces[0], plain, planes)
    b_low, b_high = spread_chain(pieces[1], swapped, planes)

    relaxed, to_near, to_far, strip = pl.pallas_call(
        functools.partial(backward_kernel, orders),
        out_shape=(
            shape((rows, cols, slices), f32),
            shape((SWEEPS * cols, slices), bf16),
            shape((SWEEPS * cols, slices), bf16),
            shape((rows, EDGE, cols), f32),
        ),
        in_specs=[HBM] * 4 + [VMEM] * 6,
        out_specs=(VMEM,) * 4,
        scratch_shapes=[
            pltpu.VMEM((parts, rays, slices), bf16),
            pltpu.VMEM((tiles + 1, voxels, slices), f32),
            *scalars,
        ],
        compiler_params=PARAMS,
        name="backward",
    )(*lists, a_low, a_high, b_low, b_high, image, held)

    other = lax.ppermute(strip, "cuts", [(0, 1), (1, 0)])
    both = jnp.where(
        cut == 0, jnp.concatenate([strip, other], 1), jnp.concatenate([other, strip], 1)
    )

    even = lax.rem(lax.axis_index("plane"), 2) == 0
    ends = both[rows - SWEEPS :], both[:SWEEPS]

    def trade(main, end_even, end_odd, pairs):
        end = jnp.where(even, end_even, end_odd).astype(bf16).reshape(-1, cols)
        return lax.ppermute(jnp.concatenate([main, end], axis=0), "plane", pairs)

    near = [(i, i ^ 1) for i in range(planes)]
    far = [(i, i + 1 if i % 2 else i - 1) for i in range(1, planes - 1)]
    from_far = trade(to_far, ends[1], ends[0], far)
    from_near = trade(to_near, ends[0], ends[1], near)

    spans = (cols, slices), (2 * EDGE, cols)
    *inner, saved, saved_strip = pl.pallas_call(
        inner_kernel,
        out_shape=[
            *(shape((rows - 2 * SWEEPS, *span), f32) for span in spans),
            *(shape((SWEEPS, 4, *span), f32) for span in spans),
        ],
        in_specs=[VMEM] * 2,
        out_specs=[VMEM] * 4,
        scratch_shapes=[pltpu.VMEM((rows, *span), f32) for span in spans],
        compiler_params=PARAMS,
        name="inner_sweeps",
    )(relaxed, both)
    volume = pl.pallas_call(
        functools.partial(edge_kernel, planes=planes),
        out_shape=shape((rows, cols, slices), f32),
        in_specs=[VMEM] * 6,
        out_specs=VMEM,
        scratch_shapes=[
            *(pltpu.VMEM((6, *span), f32) for span in spans),
            *(pltpu.VMEM((2, 6, *span), f32) for span in spans),
        ],
        compiler_params=PARAMS,
        name="edge_sweeps",
    )(*inner, saved, saved_strip, from_near, from_far)
    return (volume, residual)


def solution(mesh):
    placed = (
        P("plane", None, "cuts"),
        P("plane", None, None),
        P("plane"),
        P("plane"),
        P(),
        P("plane"),
        P("plane", None, "cuts"),
    )
    return jax.shard_map(
        per_device,
        mesh=mesh,
        in_specs=placed,
        out_specs=(P("plane", None, "cuts"), P("plane", None, "cuts")),
        check_vma=False,
    )
```

```python
import functools

import jax
import jax.numpy as jnp
from jax import lax
from jax.experimental import pallas as pl
from jax.experimental.pallas import tpu as pltpu
from jax.sharding import PartitionSpec as P

TILE = 16
SWEEPS = 4
EDGE = 8
FETCH = 8
FORWARD_GROUP = 16
BACKWARD_GROUP = 48

smooth_square = 0.09
flow_step = 0.04
relax_step = 4.0

VMEM = pl.BlockSpec(memory_space=pltpu.VMEM)
HBM = pl.BlockSpec(memory_space=pltpu.HBM)
PARAMS = pltpu.CompilerParams(vmem_limit_bytes=24 * 1024 * 1024)


def relative_block(bits, position):
    block = 0
    for stage, bit in enumerate(bits):
        block |= ((position >> (len(bits) - 1 - stage)) & 1) << bit
    return block


def weight_copy(weights, held, sems, group):
    span = pl.ds(group * FETCH, FETCH)
    return pltpu.make_async_copy(weights.at[span], held.at[span], sems.at[group])


def list_copies(lists, scalars):
    held, sem = scalars[:-1], scalars[-1]
    copies = [pltpu.make_async_copy(a, b, sem.at[i]) for i, (a, b) in enumerate(zip(lists, held))]
    for copy in copies:
        copy.start()
    return copies, held


def forward_kernel(
    orders, tile_ids, blocks, owner, count, image, weights,
    a_keep, a_send, b_keep, b_send, held, pixels, turned, total, image_sems, sems, *scalars,
):
    me = lax.axis_index("plane")
    lists, (tile_ids, blocks, owner, count) = list_copies((tile_ids, blocks, owner, count), scalars)
    slots, voxels, rays = held.shape
    parts = total.shape[0] - 1
    half = rays // 2
    tiles = turned.shape[0]
    image_copies = []
    for t in range(tiles):
        part = (slice(None), pl.ds(t * TILE, TILE))
        copy = pltpu.make_async_copy(image.at[part], pixels.at[part], image_sems.at[t])
        copy.start()
        image_copies.append(copy)
    for fetch in range(1):
        weight_copy(weights, held, sems, fetch).start()
    total[...] = jnp.zeros_like(total)
    for copy in image_copies:
        copy.wait()
    for fetch in range(1, slots // FETCH):
        weight_copy(weights, held, sems, fetch).start()
    for t in range(tiles):
        tile = pixels[:, t * TILE : (t + 1) * TILE, :].reshape(voxels, pixels.shape[2])
        turned[t] = tile.T.astype(jnp.bfloat16)
    for copy in lists:
        copy.wait()

    def step(group, carry):
        for fetch in range(FORWARD_GROUP // FETCH):
            weight_copy(weights, held, sems, group * (FORWARD_GROUP // FETCH) + fetch).wait()
        for k in range(FORWARD_GROUP):
            s = group * FORWARD_GROUP + k
            to = jnp.where(s < count[0], owner[blocks[s]] ^ me, parts)
            total[to] += jnp.dot(
                turned[tile_ids[s]], held[s], preferred_element_type=jnp.float32
            )
        return carry

    lax.fori_loop(0, slots // FORWARD_GROUP, step, 0)
    for keep, send, order, low in ((a_keep, a_send, orders[0], 0), (b_keep, b_send, orders[1], half)):
        for p in range(parts // 2):
            keep[p] = total[relative_block(order, p), :, low : low + half]
            send[p] = total[relative_block(order, p + parts // 2), :, low : low + half].astype(jnp.bfloat16)


def residual_kernel(low, keep, got, measured, residual):
    half = residual.shape[1]
    projection = (keep[0] + got[0].astype(jnp.float32)).T
    mismatch = measured[0, low : low + half, :] - projection
    residual[0] = (mismatch / jnp.sqrt(1.0 + mismatch * mismatch)).astype(jnp.bfloat16)


def backward_kernel(
    orders, tile_ids, blocks, owner, count, a_low, a_high, b_low, b_high, image, weights,
    relaxed, to_near, to_far, strip, spread, total, *scalars,
):
    me = lax.axis_index("plane")
    cut = lax.axis_index("cuts")
    lists, (tile_ids, blocks, owner, count) = list_copies((tile_ids, blocks, owner, count), scalars)
    slots, voxels, rays = weights.shape
    parts = spread.shape[0]
    tiles = total.shape[0] - 1
    half = rays // 2
    rows, cols, slices = relaxed.shape
    total[...] = jnp.zeros_like(total)
    for p in range(parts // 2):
        spread[relative_block(orders[0], p), :half] = a_low[p]
        spread[relative_block(orders[0], p + parts // 2), :half] = a_high[p]
        spread[relative_block(orders[1], p), half:] = b_low[p]
        spread[relative_block(orders[1], p + parts // 2), half:] = b_high[p]

    for copy in lists:
        copy.wait()

    def step(group, carry):
        for k in range(BACKWARD_GROUP):
            s = group * BACKWARD_GROUP + k
            to = jnp.where(s < count[0], tile_ids[s], tiles)
            total[to] += jnp.dot(
                weights[s], spread[owner[blocks[s]] ^ me], preferred_element_type=jnp.float32
            )
        return carry

    lax.fori_loop(0, slots // BACKWARD_GROUP, step, 0)
    for t in range(tiles):
        span = slice(t * TILE, (t + 1) * TILE)
        update = total[t].reshape(rows, TILE, slices)
        relaxed[:, span, :] = jnp.maximum(image[:, span, :] + relax_step * update, 0.0)
    even = lax.rem(me, 2) == 0
    for side, start in (
        (to_near, jnp.where(even, rows - SWEEPS, 0)),
        (to_far, jnp.where(even, 0, rows - SWEEPS)),
    ):
        for i in range(SWEEPS):
            side[i * cols : (i + 1) * cols] = relaxed[start + i].astype(jnp.bfloat16)
    lane = lax.broadcasted_iota(jnp.int32, (cols, slices), 1)
    start = jnp.where(cut == 0, slices - EDGE, 0)
    edges = jnp.zeros((cols, slices), jnp.float32)
    for i in range(rows):
        moved = pltpu.roll(relaxed[i], (i * EDGE - start + slices) % slices, 1)
        edges = jnp.where(lane // EDGE == i, moved, edges)
    strip[...] = edges.T.reshape(rows, EDGE, cols)


def shifted(x, axis, by):
    size = x.shape[axis]
    place = lax.broadcasted_iota(jnp.int32, x.shape, axis)
    if by > 0:
        return jnp.where(place == 0, 0.0, pltpu.roll(x, 1, axis))
    return jnp.where(place == size - 1, 0.0, pltpu.roll(x, size - 1, axis))


def flows(cell, below):
    rise_rows = below - cell
    rise_inner = shifted(cell, 0, -1) - cell
    rise_outer = shifted(cell, 1, -1) - cell
    scale = lax.rsqrt(
        smooth_square + rise_rows * rise_rows + rise_inner * rise_inner + rise_outer * rise_outer
    )
    return rise_rows * scale, rise_inner * scale, rise_outer * scale


def advance(cell, below, before):
    flow_rows, flow_inner, flow_outer = flows(cell, below)
    diverge = flow_rows - before
    diverge = diverge + (flow_inner - shifted(flow_inner, 0, 1))
    diverge = diverge + (flow_outer - shifted(flow_outer, 1, 1))
    return cell + flow_step * diverge, flow_rows


def patched(rows, strips, cut):
    count, _, cols = strips.shape
    slices = rows[0].shape[1]
    low_side = cut == 0
    mine = jnp.where(low_side, strips[:, :EDGE], strips[:, EDGE:]).reshape(count * EDGE, cols)
    turned = jnp.concatenate([mine] * (slices // (count * EDGE)), axis=0).T
    lane = lax.broadcasted_iota(jnp.int32, (cols, slices), 1)
    start = jnp.where(low_side, slices - EDGE, 0)
    first = jnp.where(low_side, slices - SWEEPS, 0)
    patch = (lane >= first) & (lane < first + SWEEPS)
    return [
        jnp.where(patch, pltpu.roll(turned, (start - i * EDGE + slices) % slices, 1), row)
        for i, row in enumerate(rows)
    ]


def inner_kernel(relaxed, strip, *refs):
    rows = relaxed.shape[0]
    result, saves, fields = refs[0], refs[1:3], refs[3:5]
    for field, start in zip(fields, (relaxed, strip)):
        field[...] = start[...]
    for k in range(SWEEPS):
        for field, save in zip(fields, saves):
            save[k, 0:2] = field[k : k + 2]
            save[k, 2:4] = field[rows - 2 - k : rows - k]

        def body(i, before):
            after = []
            for field, flow in zip(fields, before):
                field[i], flow = advance(field[i], field[i + 1], flow)
                after.append(flow)
            return tuple(after)

        before = tuple(flows(field[k], field[k + 1])[0] for field in fields)
        lax.fori_loop(k + 1, rows - 1 - k, body, before, unroll=3)
    inner = [fields[0][i] for i in range(SWEEPS, rows - SWEEPS)]
    strips = fields[1][SWEEPS : rows - SWEEPS]
    for i, row in enumerate(patched(inner, strips, lax.axis_index("cuts"))):
        result[i] = row


def edge_kernel(
    inner, saved, saved_strip, from_near, from_far, volume,
    low_field, low_strip, high_field, high_strip, ends, sems, *, planes,
):
    rows, cols, slices = volume.shape
    me, cut = lax.axis_index("plane"), lax.axis_index("cuts")
    inner_copy = pltpu.make_async_copy(inner, volume.at[pl.ds(SWEEPS, rows - 2 * SWEEPS)], sems.at[0])
    inner_copy.start()
    body_rows = SWEEPS * cols
    even = lax.rem(me, 2) == 0
    for other, this, field, strip, at in (
        (from_near, from_far, low_field, low_strip, (slice(0, 4),)),
        (from_far, from_near, high_field, high_strip, (0, slice(2, 6))),
    ):
        halo = jnp.where(even, this[...], other[...])
        field[at] = halo[:body_rows].astype(jnp.float32).reshape(SWEEPS, cols, slices)
        strip[at] = halo[body_rows:].astype(jnp.float32).reshape(SWEEPS, 2 * EDGE, cols)
    pairs = ((low_field, high_field, saved), (low_strip, high_strip, saved_strip))
    for k in range(SWEEPS):
        now, later = k % 2, (k + 1) % 2
        for low, high, save in pairs:
            low[4:6] = save[k, 0:2]
            high[now, 0:2] = save[k, 2:4]

        @pl.when(me == 0)
        def _():
            for low, _, _ in pairs:
                low[3 - k] = low[4 - k]

        @pl.when(me == planes - 1)
        def _():
            for _, high, _ in pairs:
                high[now, 2 + k] = jnp.zeros(high.shape[2:], high.dtype)

        def body(i, before):
            after = []
            for (low, high, _), (flow_low, flow_high) in zip(pairs, before):
                low[i - 1], flow_low = advance(low[i], low[i + 1], flow_low)
                high[later, i + 1], flow_high = advance(high[now, i], high[now, i + 1], flow_high)
                after.append((flow_low, flow_high))
            return tuple(after)

        before = tuple(
            (flows(low[0], low[1])[0], flows(high[now, 0], high[now, 1])[0]) for low, high, _ in pairs
        )
        lax.fori_loop(1, SWEEPS + 1, body, before, unroll=2)
    last = SWEEPS % 2
    outer = [low_field[i] for i in range(SWEEPS)] + [high_field[last, 2 + i] for i in range(SWEEPS)]
    strips = jnp.concatenate([low_strip[0:4], high_strip[last, 2:6]], axis=0)
    for i, row in enumerate(patched(outer, strips, cut)):
        ends[i] = row
    copies = [
        inner_copy,
        pltpu.make_async_copy(ends.at[pl.ds(0, SWEEPS)], volume.at[pl.ds(0, SWEEPS)], sems.at[1]),
        pltpu.make_async_copy(ends.at[pl.ds(SWEEPS, SWEEPS)], volume.at[pl.ds(rows - SWEEPS, SWEEPS)], sems.at[2]),
    ]
    for copy in copies[1:]:
        copy.start()
    for copy in copies:
        copy.wait()


def sum_chain(keep, send, order, planes):
    for stage, bit in enumerate(order):
        got = lax.ppermute(send, "plane", [(i, i ^ (1 << bit)) for i in range(planes)])
        if stage == len(order) - 1:
            return keep, got
        total = keep + got.astype(jnp.float32)
        left = total.shape[0] // 2
        keep, send = total[:left], total[left:].astype(jnp.bfloat16)


def spread_chain(piece, order, planes):
    for stage, bit in reversed(list(enumerate(order))):
        got = lax.ppermute(piece, "plane", [(i, i ^ (1 << bit)) for i in range(planes)])
        if stage == 0:
            return piece, got
        piece = jnp.concatenate([piece, got], axis=0)


def per_device(
    image,
    projection_weight_tiles,
    pair_tile_index,
    pair_ray_block,
    ray_owner,
    active_pair_count,
    measured,
):
    rows, cols, slices = image.shape
    slots, voxels, rays = projection_weight_tiles.shape
    tiles = (rows // TILE) * (cols // TILE)
    planes = lax.axis_size("plane")
    parts = ray_owner.shape[0]
    half = rays // 2
    bits = planes.bit_length() - 1
    plain = tuple(range(bits))
    swapped = (1, 0) + plain[2:]
    orders = (plain, swapped)
    cut = lax.axis_index("cuts")
    shape = jax.ShapeDtypeStruct
    f32, bf16 = jnp.float32, jnp.bfloat16

    weights = pltpu.with_memory_space_constraint(projection_weight_tiles, pltpu.HBM)
    lists = [
        pltpu.with_memory_space_constraint(a, pltpu.HBM)
        for a in (pair_tile_index, pair_ray_block, ray_owner)
    ] + [active_pair_count]
    far_image = pltpu.with_memory_space_constraint(image, pltpu.HBM)
    scalars = [
        *(pltpu.SMEM(a.shape, jnp.int32) for a in lists),
        pltpu.SemaphoreType.DMA((4,)),
    ]

    kept, sent = shape((parts // 2, slices, half), f32), shape((parts // 2, slices, half), bf16)
    a_keep, a_send, b_keep, b_send, held, pixels = pl.pallas_call(
        functools.partial(forward_kernel, orders),
        out_shape=(kept, sent, kept, sent, shape(weights.shape, bf16), shape(image.shape, f32)),
        in_specs=[HBM] * 6,
        out_specs=(VMEM,) * 6,
        scratch_shapes=[
            pltpu.VMEM((tiles, slices, voxels), bf16),
            pltpu.VMEM((parts + 1, slices, rays), f32),
            pltpu.SemaphoreType.DMA((tiles,)),
            pltpu.SemaphoreType.DMA((slots // FETCH,)),
            *scalars,
        ],
        compiler_params=PARAMS,
        name="forward",
    )(*lists, far_image, weights)

    pieces = []
    for low, keep, send, order in ((0, a_keep, a_send, plain), (half, b_keep, b_send, swapped)):
        keep, got = sum_chain(keep, send, order, planes)
        pieces.append(
            pl.pallas_call(
                functools.partial(residual_kernel, low),
                out_shape=shape((1, half, slices), bf16),
                in_specs=[VMEM] * 3,
                out_specs=VMEM,
                compiler_params=PARAMS,
                name="residual",
            )(keep, got, measured)
        )
    residual = jnp.concatenate(pieces, axis=1)
    a_low, a_high = spread_chain(pieces[0], plain, planes)
    b_low, b_high = spread_chain(pieces[1], swapped, planes)

    relaxed, to_near, to_far, strip = pl.pallas_call(
        functools.partial(backward_kernel, orders),
        out_shape=(
            shape((rows, cols, slices), f32),
            shape((SWEEPS * cols, slices), bf16),
            shape((SWEEPS * cols, slices), bf16),
            shape((rows, EDGE, cols), f32),
        ),
        in_specs=[HBM] * 4 + [VMEM] * 6,
        out_specs=(VMEM,) * 4,
        scratch_shapes=[
            pltpu.VMEM((parts, rays, slices), bf16),
            pltpu.VMEM((tiles + 1, voxels, slices), f32),
            *scalars,
        ],
        compiler_params=PARAMS,
        name="backward",
    )(*lists, a_low, a_high, b_low, b_high, pixels, held)

    other = lax.ppermute(strip, "cuts", [(0, 1), (1, 0)])
    both = jnp.where(
        cut == 0, jnp.concatenate([strip, other], 1), jnp.concatenate([other, strip], 1)
    )

    even = lax.rem(lax.axis_index("plane"), 2) == 0
    ends = both[rows - SWEEPS :], both[:SWEEPS]

    def trade(main, end_even, end_odd, pairs):
        end = jnp.where(even, end_even, end_odd).astype(bf16).reshape(-1, cols)
        return lax.ppermute(jnp.concatenate([main, end], axis=0), "plane", pairs)

    near = [(i, i ^ 1) for i in range(planes)]
    far = [(i, i + 1 if i % 2 else i - 1) for i in range(1, planes - 1)]
    from_far = trade(to_far, ends[1], ends[0], far)
    from_near = trade(to_near, ends[0], ends[1], near)

    spans = (cols, slices), (2 * EDGE, cols)
    inner, saved, saved_strip = pl.pallas_call(
        inner_kernel,
        out_shape=[
            shape((rows - 2 * SWEEPS, cols, slices), f32),
            *(shape((SWEEPS, 4, *span), f32) for span in spans),
        ],
        in_specs=[VMEM] * 2,
        out_specs=[VMEM] * 3,
        scratch_shapes=[pltpu.VMEM((rows, *span), f32) for span in spans],
        compiler_params=PARAMS,
        name="inner_sweeps",
    )(relaxed, both)
    volume = pl.pallas_call(
        functools.partial(edge_kernel, planes=planes),
        out_shape=shape((rows, cols, slices), f32),
        in_specs=[VMEM] * 5,
        out_specs=HBM,
        scratch_shapes=[
            *(pltpu.VMEM((6, *span), f32) for span in spans),
            *(pltpu.VMEM((2, 6, *span), f32) for span in spans),
            pltpu.VMEM((2 * SWEEPS, cols, slices), f32),
            pltpu.SemaphoreType.DMA((3,)),
        ],
        compiler_params=PARAMS,
        name="edge_sweeps",
    )(inner, saved, saved_strip, from_near, from_far)
    return (volume, residual)


def solution(mesh):
    placed = (
        P("plane", None, "cuts"),
        P("plane", None, None),
        P("plane"),
        P("plane"),
        P(),
        P("plane"),
        P("plane", None, "cuts"),
    )
    return jax.shard_map(
        per_device,
        mesh=mesh,
        in_specs=placed,
        out_specs=(P("plane", None, "cuts"), P("plane", None, "cuts")),
        check_vma=False,
    )
```

```python
import functools

import jax
import jax.numpy as jnp
from jax import lax
from jax.experimental import pallas as pl
from jax.experimental.pallas import tpu as pltpu
from jax.sharding import PartitionSpec as P

TILE = 16
SWEEPS = 4
EDGE = 8
FETCH = 8
FORWARD_GROUP = 16
BACKWARD_GROUP = 48

smooth_square = 0.09
flow_step = 0.04
relax_step = 4.0

VMEM = pl.BlockSpec(memory_space=pltpu.VMEM)
HBM = pl.BlockSpec(memory_space=pltpu.HBM)
PARAMS = pltpu.CompilerParams(vmem_limit_bytes=24 * 1024 * 1024)


def relative_block(bits, position):
    block = 0
    for stage, bit in enumerate(bits):
        block |= ((position >> (len(bits) - 1 - stage)) & 1) << bit
    return block


def weight_copy(weights, held, sems, group):
    span = pl.ds(group * FETCH, FETCH)
    return pltpu.make_async_copy(weights.at[span], held.at[span], sems.at[group])


def list_copies(lists, scalars):
    held, sem = scalars[:-1], scalars[-1]
    copies = [pltpu.make_async_copy(a, b, sem.at[i]) for i, (a, b) in enumerate(zip(lists, held))]
    for copy in copies:
        copy.start()
    return copies, held


def forward_kernel(
    orders, tile_ids, blocks, owner, count, image, weights,
    a_keep, a_send, b_keep, b_send, held, pixels, turned, total, image_sems, sems, *scalars,
):
    me = lax.axis_index("plane")
    lists, (tile_ids, blocks, owner, count) = list_copies((tile_ids, blocks, owner, count), scalars)
    slots, voxels, rays = held.shape
    parts = total.shape[0] - 1
    half = rays // 2
    tiles = turned.shape[0]
    image_copies = []
    for t in range(tiles):
        part = (slice(None), pl.ds(t * TILE, TILE))
        copy = pltpu.make_async_copy(image.at[part], pixels.at[part], image_sems.at[t])
        copy.start()
        image_copies.append(copy)
    for fetch in range(1):
        weight_copy(weights, held, sems, fetch).start()
    total[...] = jnp.zeros_like(total)
    for copy in image_copies:
        copy.wait()
    for fetch in range(1, slots // FETCH):
        weight_copy(weights, held, sems, fetch).start()
    for t in range(tiles):
        tile = pixels[:, t * TILE : (t + 1) * TILE, :].reshape(voxels, pixels.shape[2])
        turned[t] = tile.T.astype(jnp.bfloat16)
    for copy in lists:
        copy.wait()

    def step(group, carry):
        for fetch in range(FORWARD_GROUP // FETCH):
            weight_copy(weights, held, sems, group * (FORWARD_GROUP // FETCH) + fetch).wait()
        for k in range(FORWARD_GROUP):
            s = group * FORWARD_GROUP + k
            to = jnp.where(s < count[0], owner[blocks[s]] ^ me, parts)
            total[to] += jnp.dot(
                turned[tile_ids[s]], held[s], preferred_element_type=jnp.float32
            )
        return carry

    lax.fori_loop(0, slots // FORWARD_GROUP, step, 0)
    for keep, send, order, low in ((a_keep, a_send, orders[0], 0), (b_keep, b_send, orders[1], half)):
        for p in range(parts // 2):
            keep[p] = total[relative_block(order, p), :, low : low + half]
            send[p] = total[relative_block(order, p + parts // 2), :, low : low + half].astype(jnp.bfloat16)


def residual_kernel(low, total, got, measured, measured_other, residual):
    half = residual.shape[1]
    for p, target in enumerate((measured[0, low : low + half, :], measured_other[0])):
        projection = (total[p] + got[1 - p].astype(jnp.float32)).T
        mismatch = target - projection
        residual[p] = (mismatch / jnp.sqrt(1.0 + mismatch * mismatch)).astype(jnp.bfloat16)


def backward_kernel(
    orders, tile_ids, blocks, owner, count, a_low, a_high, b_low, b_high, image, weights,
    relaxed, to_near, to_far, strip, spread, total, *scalars,
):
    me = lax.axis_index("plane")
    cut = lax.axis_index("cuts")
    lists, (tile_ids, blocks, owner, count) = list_copies((tile_ids, blocks, owner, count), scalars)
    slots, voxels, rays = weights.shape
    parts = spread.shape[0]
    tiles = total.shape[0] - 1
    half = rays // 2
    rows, cols, slices = relaxed.shape
    total[...] = jnp.zeros_like(total)
    for p in range(parts // 2):
        spread[relative_block(orders[0], p), :half] = a_low[p]
        spread[relative_block(orders[0], p + parts // 2), :half] = a_high[p]
        spread[relative_block(orders[1], p), half:] = b_low[p]
        spread[relative_block(orders[1], p + parts // 2), half:] = b_high[p]

    for copy in lists:
        copy.wait()

    def step(group, carry):
        for k in range(BACKWARD_GROUP):
            s = group * BACKWARD_GROUP + k
            to = jnp.where(s < count[0], tile_ids[s], tiles)
            total[to] += jnp.dot(
                weights[s], spread[owner[blocks[s]] ^ me], preferred_element_type=jnp.float32
            )
        return carry

    lax.fori_loop(0, slots // BACKWARD_GROUP, step, 0)
    for t in range(tiles):
        span = slice(t * TILE, (t + 1) * TILE)
        update = total[t].reshape(rows, TILE, slices)
        relaxed[:, span, :] = jnp.maximum(image[:, span, :] + relax_step * update, 0.0)
    even = lax.rem(me, 2) == 0
    for side, start in (
        (to_near, jnp.where(even, rows - SWEEPS, 0)),
        (to_far, jnp.where(even, 0, rows - SWEEPS)),
    ):
        for i in range(SWEEPS):
            side[i * cols : (i + 1) * cols] = relaxed[start + i].astype(jnp.bfloat16)
    lane = lax.broadcasted_iota(jnp.int32, (cols, slices), 1)
    start = jnp.where(cut == 0, slices - EDGE, 0)
    edges = jnp.zeros((cols, slices), jnp.float32)
    for i in range(rows):
        moved = pltpu.roll(relaxed[i], (i * EDGE - start + slices) % slices, 1)
        edges = jnp.where(lane // EDGE == i, moved, edges)
    strip[...] = edges.T.reshape(rows, EDGE, cols)


def shifted(x, axis, by):
    size = x.shape[axis]
    place = lax.broadcasted_iota(jnp.int32, x.shape, axis)
    if by > 0:
        return jnp.where(place == 0, 0.0, pltpu.roll(x, 1, axis))
    return jnp.where(place == size - 1, 0.0, pltpu.roll(x, size - 1, axis))


def flows(cell, below):
    rise_rows = below - cell
    rise_inner = shifted(cell, 0, -1) - cell
    rise_outer = shifted(cell, 1, -1) - cell
    scale = lax.rsqrt(
        smooth_square + rise_rows * rise_rows + rise_inner * rise_inner + rise_outer * rise_outer
    )
    return rise_rows * scale, rise_inner * scale, rise_outer * scale


def advance(cell, below, before):
    flow_rows, flow_inner, flow_outer = flows(cell, below)
    diverge = flow_rows - before
    diverge = diverge + (flow_inner - shifted(flow_inner, 0, 1))
    diverge = diverge + (flow_outer - shifted(flow_outer, 1, 1))
    return cell + flow_step * diverge, flow_rows


def patched(rows, strips, cut):
    count, _, cols = strips.shape
    slices = rows[0].shape[1]
    low_side = cut == 0
    mine = jnp.where(low_side, strips[:, :EDGE], strips[:, EDGE:]).reshape(count * EDGE, cols)
    turned = jnp.concatenate([mine] * (slices // (count * EDGE)), axis=0).T
    lane = lax.broadcasted_iota(jnp.int32, (cols, slices), 1)
    start = jnp.where(low_side, slices - EDGE, 0)
    first = jnp.where(low_side, slices - SWEEPS, 0)
    patch = (lane >= first) & (lane < first + SWEEPS)
    return [
        jnp.where(patch, pltpu.roll(turned, (start - i * EDGE + slices) % slices, 1), row)
        for i, row in enumerate(rows)
    ]


def inner_kernel(relaxed, strip, *refs):
    rows = relaxed.shape[0]
    result, saves, fields = refs[0], refs[1:3], refs[3:5]
    for field, start in zip(fields, (relaxed, strip)):
        field[...] = start[...]
    for k in range(SWEEPS):
        for field, save in zip(fields, saves):
            save[k, 0:2] = field[k : k + 2]
            save[k, 2:4] = field[rows - 2 - k : rows - k]

        def body(i, before):
            after = []
            for field, flow in zip(fields, before):
                field[i], flow = advance(field[i], field[i + 1], flow)
                after.append(flow)
            return tuple(after)

        before = tuple(flows(field[k], field[k + 1])[0] for field in fields)
        lax.fori_loop(k + 1, rows - 1 - k, body, before, unroll=3)
    inner = [fields[0][i] for i in range(SWEEPS, rows - SWEEPS)]
    strips = fields[1][SWEEPS : rows - SWEEPS]
    for i, row in enumerate(patched(inner, strips, lax.axis_index("cuts"))):
        result[i] = row


def edge_kernel(
    inner, saved, saved_strip, from_near, from_far, volume,
    low_field, low_strip, high_field, high_strip, ends, sems, *, planes,
):
    rows, cols, slices = volume.shape
    me, cut = lax.axis_index("plane"), lax.axis_index("cuts")
    inner_copy = pltpu.make_async_copy(inner, volume.at[pl.ds(SWEEPS, rows - 2 * SWEEPS)], sems.at[0])
    inner_copy.start()
    body_rows = SWEEPS * cols
    even = lax.rem(me, 2) == 0
    for other, this, field, strip, at in (
        (from_near, from_far, low_field, low_strip, (slice(0, 4),)),
        (from_far, from_near, high_field, high_strip, (0, slice(2, 6))),
    ):
        halo = jnp.where(even, this[...], other[...])
        field[at] = halo[:body_rows].astype(jnp.float32).reshape(SWEEPS, cols, slices)
        strip[at] = halo[body_rows:].astype(jnp.float32).reshape(SWEEPS, 2 * EDGE, cols)
    pairs = ((low_field, high_field, saved), (low_strip, high_strip, saved_strip))
    for k in range(SWEEPS):
        now, later = k % 2, (k + 1) % 2
        for low, high, save in pairs:
            low[4:6] = save[k, 0:2]
            high[now, 0:2] = save[k, 2:4]

        @pl.when(me == 0)
        def _():
            for low, _, _ in pairs:
                low[3 - k] = low[4 - k]

        @pl.when(me == planes - 1)
        def _():
            for _, high, _ in pairs:
                high[now, 2 + k] = jnp.zeros(high.shape[2:], high.dtype)

        def body(i, before):
            after = []
            for (low, high, _), (flow_low, flow_high) in zip(pairs, before):
                low[i - 1], flow_low = advance(low[i], low[i + 1], flow_low)
                high[later, i + 1], flow_high = advance(high[now, i], high[now, i + 1], flow_high)
                after.append((flow_low, flow_high))
            return tuple(after)

        before = tuple(
            (flows(low[0], low[1])[0], flows(high[now, 0], high[now, 1])[0]) for low, high, _ in pairs
        )
        lax.fori_loop(1, SWEEPS + 1, body, before, unroll=2)
    last = SWEEPS % 2
    outer = [low_field[i] for i in range(SWEEPS)] + [high_field[last, 2 + i] for i in range(SWEEPS)]
    strips = jnp.concatenate([low_strip[0:4], high_strip[last, 2:6]], axis=0)
    for i, row in enumerate(patched(outer, strips, cut)):
        ends[i] = row
    copies = [
        inner_copy,
        pltpu.make_async_copy(ends.at[pl.ds(0, SWEEPS)], volume.at[pl.ds(0, SWEEPS)], sems.at[1]),
        pltpu.make_async_copy(ends.at[pl.ds(SWEEPS, SWEEPS)], volume.at[pl.ds(rows - SWEEPS, SWEEPS)], sems.at[2]),
    ]
    for copy in copies[1:]:
        copy.start()
    for copy in copies:
        copy.wait()


def partner(bit, planes):
    return [(i, i ^ (1 << bit)) for i in range(planes)]


def sum_chain(keep, send, order, planes):
    for bit in order[:-1]:
        got = lax.ppermute(send, "plane", partner(bit, planes))
        total = keep + got.astype(jnp.float32)
        left = total.shape[0] // 2
        keep, send = total[:left], total[left:].astype(jnp.bfloat16)
    return total, lax.ppermute(total.astype(jnp.bfloat16), "plane", partner(order[-1], planes))


def spread_chain(piece, order, planes):
    for bit in reversed(order[1:-1]):
        got = lax.ppermute(piece, "plane", partner(bit, planes))
        piece = jnp.concatenate([piece, got], axis=0)
    return piece, lax.ppermute(piece, "plane", partner(order[0], planes))


def per_device(
    image,
    projection_weight_tiles,
    pair_tile_index,
    pair_ray_block,
    ray_owner,
    active_pair_count,
    measured,
):
    rows, cols, slices = image.shape
    slots, voxels, rays = projection_weight_tiles.shape
    tiles = (rows // TILE) * (cols // TILE)
    planes = lax.axis_size("plane")
    parts = ray_owner.shape[0]
    half = rays // 2
    bits = planes.bit_length() - 1
    plain = tuple(range(bits))
    swapped = (1, 0) + plain[2:]
    orders = (plain, swapped)
    cut = lax.axis_index("cuts")
    shape = jax.ShapeDtypeStruct
    f32, bf16 = jnp.float32, jnp.bfloat16

    weights = pltpu.with_memory_space_constraint(projection_weight_tiles, pltpu.HBM)
    lists = [
        pltpu.with_memory_space_constraint(a, pltpu.HBM)
        for a in (pair_tile_index, pair_ray_block, ray_owner)
    ] + [active_pair_count]
    far_image = pltpu.with_memory_space_constraint(image, pltpu.HBM)
    scalars = [
        *(pltpu.SMEM(a.shape, jnp.int32) for a in lists),
        pltpu.SemaphoreType.DMA((4,)),
    ]

    kept, sent = shape((parts // 2, slices, half), f32), shape((parts // 2, slices, half), bf16)
    a_keep, a_send, b_keep, b_send, held, pixels = pl.pallas_call(
        functools.partial(forward_kernel, orders),
        out_shape=(kept, sent, kept, sent, shape(weights.shape, bf16), shape(image.shape, f32)),
        in_specs=[HBM] * 6,
        out_specs=(VMEM,) * 6,
        scratch_shapes=[
            pltpu.VMEM((tiles, slices, voxels), bf16),
            pltpu.VMEM((parts + 1, slices, rays), f32),
            pltpu.SemaphoreType.DMA((tiles,)),
            pltpu.SemaphoreType.DMA((slots // FETCH,)),
            *scalars,
        ],
        compiler_params=PARAMS,
        name="forward",
    )(*lists, far_image, weights)

    b_keep, target = lax.optimization_barrier((b_keep, measured))
    pieces = []
    for low, keep, send, order in ((0, a_keep, a_send, plain), (half, b_keep, b_send, swapped)):
        target_other = lax.ppermute(target[:, low : low + half], "plane", partner(order[-1], planes))
        total, got = sum_chain(keep, send, order, planes)
        pieces.append(
            pl.pallas_call(
                functools.partial(residual_kernel, low),
                out_shape=shape((2, half, slices), bf16),
                in_specs=[VMEM] * 4,
                out_specs=VMEM,
                compiler_params=PARAMS,
                name="residual",
            )(total, got, measured, target_other)
        )
    residual = jnp.concatenate([piece[:1] for piece in pieces], axis=1)
    a_low, a_high = spread_chain(pieces[0], plain, planes)
    b_low, b_high = spread_chain(pieces[1], swapped, planes)

    relaxed, to_near, to_far, strip = pl.pallas_call(
        functools.partial(backward_kernel, orders),
        out_shape=(
            shape((rows, cols, slices), f32),
            shape((SWEEPS * cols, slices), bf16),
            shape((SWEEPS * cols, slices), bf16),
            shape((rows, EDGE, cols), f32),
        ),
        in_specs=[HBM] * 4 + [VMEM] * 6,
        out_specs=(VMEM,) * 4,
        scratch_shapes=[
            pltpu.VMEM((parts, rays, slices), bf16),
            pltpu.VMEM((tiles + 1, voxels, slices), f32),
            *scalars,
        ],
        compiler_params=PARAMS,
        name="backward",
    )(*lists, a_low, a_high, b_low, b_high, pixels, held)

    other = lax.ppermute(strip, "cuts", [(0, 1), (1, 0)])
    both = jnp.where(
        cut == 0, jnp.concatenate([strip, other], 1), jnp.concatenate([other, strip], 1)
    )

    even = lax.rem(lax.axis_index("plane"), 2) == 0
    ends = both[rows - SWEEPS :], both[:SWEEPS]

    def trade(main, end_even, end_odd, pairs):
        end = jnp.where(even, end_even, end_odd).astype(bf16).reshape(-1, cols)
        return lax.ppermute(jnp.concatenate([main, end], axis=0), "plane", pairs)

    near = [(i, i ^ 1) for i in range(planes)]
    far = [(i, i + 1 if i % 2 else i - 1) for i in range(1, planes - 1)]
    from_far = trade(to_far, ends[1], ends[0], far)
    from_near = trade(to_near, ends[0], ends[1], near)

    spans = (cols, slices), (2 * EDGE, cols)
    inner, saved, saved_strip = pl.pallas_call(
        inner_kernel,
        out_shape=[
            shape((rows - 2 * SWEEPS, cols, slices), f32),
            *(shape((SWEEPS, 4, *span), f32) for span in spans),
        ],
        in_specs=[VMEM] * 2,
        out_specs=[VMEM] * 3,
        scratch_shapes=[pltpu.VMEM((rows, *span), f32) for span in spans],
        compiler_params=PARAMS,
        name="inner_sweeps",
    )(relaxed, both)
    volume = pl.pallas_call(
        functools.partial(edge_kernel, planes=planes),
        out_shape=shape((rows, cols, slices), f32),
        in_specs=[VMEM] * 5,
        out_specs=HBM,
        scratch_shapes=[
            *(pltpu.VMEM((6, *span), f32) for span in spans),
            *(pltpu.VMEM((2, 6, *span), f32) for span in spans),
            pltpu.VMEM((2 * SWEEPS, cols, slices), f32),
            pltpu.SemaphoreType.DMA((3,)),
        ],
        compiler_params=PARAMS,
        name="edge_sweeps",
    )(inner, saved, saved_strip, from_near, from_far)
    return (volume, residual)


def solution(mesh):
    placed = (
        P("plane", None, "cuts"),
        P("plane", None, None),
        P("plane"),
        P("plane"),
        P(),
        P("plane"),
        P("plane", None, "cuts"),
    )
    return jax.shard_map(
        per_device,
        mesh=mesh,
        in_specs=placed,
        out_specs=(P("plane", None, "cuts"), P("plane", None, "cuts")),
        check_vma=False,
    )
```

```python
import functools

import jax
import jax.numpy as jnp
from jax import lax
from jax.experimental import pallas as pl
from jax.experimental.pallas import tpu as pltpu
from jax.sharding import PartitionSpec as P

TILE = 16
SWEEPS = 4
EDGE = 8
FETCH = 8
FORWARD_GROUP = 16
BACKWARD_GROUP = 48

smooth_square = 0.09
flow_step = 0.04
relax_step = 4.0

VMEM = pl.BlockSpec(memory_space=pltpu.VMEM)
HBM = pl.BlockSpec(memory_space=pltpu.HBM)
PARAMS = pltpu.CompilerParams(vmem_limit_bytes=24 * 1024 * 1024)


def relative_block(bits, position):
    block = 0
    for stage, bit in enumerate(bits):
        block |= ((position >> (len(bits) - 1 - stage)) & 1) << bit
    return block


def weight_copy(weights, held, sems, group):
    span = pl.ds(group * FETCH, FETCH)
    return pltpu.make_async_copy(weights.at[span], held.at[span], sems.at[group])


def list_copies(lists, scalars):
    held, sem = scalars[:-1], scalars[-1]
    copies = [pltpu.make_async_copy(a, b, sem.at[i]) for i, (a, b) in enumerate(zip(lists, held))]
    for copy in copies:
        copy.start()
    return copies, held


def forward_kernel(
    orders, tile_ids, blocks, owner, count, image, weights,
    a_keep, a_send, b_keep, b_send, held, pixels, turned, total, image_sems, sems, *scalars,
):
    me = lax.axis_index("plane")
    lists, (tile_ids, blocks, owner, count) = list_copies((tile_ids, blocks, owner, count), scalars)
    slots, voxels, rays = held.shape
    parts = total.shape[0] - 1
    half = rays // 2
    tiles = turned.shape[0]
    image_copies = []
    for t in range(tiles):
        part = (slice(None), pl.ds(t * TILE, TILE))
        copy = pltpu.make_async_copy(image.at[part], pixels.at[part], image_sems.at[t])
        copy.start(priority=0)
        image_copies.append(copy)
    for fetch in range(12):
        weight_copy(weights, held, sems, fetch).start(priority=1)
    total[...] = jnp.zeros_like(total)
    for copy in image_copies:
        copy.wait()
    for fetch in range(12, slots // FETCH):
        weight_copy(weights, held, sems, fetch).start(priority=1)
    for t in range(tiles):
        tile = pixels[:, t * TILE : (t + 1) * TILE, :].reshape(voxels, pixels.shape[2])
        turned[t] = tile.T.astype(jnp.bfloat16)
    for copy in lists:
        copy.wait()

    def step(group, carry):
        for fetch in range(FORWARD_GROUP // FETCH):
            weight_copy(weights, held, sems, group * (FORWARD_GROUP // FETCH) + fetch).wait()
        for k in range(FORWARD_GROUP):
            s = group * FORWARD_GROUP + k
            to = jnp.where(s < count[0], owner[blocks[s]] ^ me, parts)
            total[to] += jnp.dot(
                turned[tile_ids[s]], held[s], preferred_element_type=jnp.float32
            )
        return carry

    lax.fori_loop(0, slots // FORWARD_GROUP, step, 0)
    for keep, send, order, low in ((a_keep, a_send, orders[0], 0), (b_keep, b_send, orders[1], half)):
        for p in range(parts // 2):
            keep[p] = total[relative_block(order, p), :, low : low + half]
            send[p] = total[relative_block(order, p + parts // 2), :, low : low + half].astype(jnp.bfloat16)


def residual_kernel(low, total, got, measured, measured_other, residual):
    half = residual.shape[1]
    for p, target in enumerate((measured[0, low : low + half, :], measured_other[0])):
        projection = (total[p] + got[1 - p].astype(jnp.float32)).T
        mismatch = target - projection
        residual[p] = (mismatch / jnp.sqrt(1.0 + mismatch * mismatch)).astype(jnp.bfloat16)


def backward_kernel(
    orders, tile_ids, blocks, owner, count, a_low, a_high, b_low, b_high, image, weights,
    relaxed, to_near, to_far, strip, spread, total, *scalars,
):
    me = lax.axis_index("plane")
    cut = lax.axis_index("cuts")
    lists, (tile_ids, blocks, owner, count) = list_copies((tile_ids, blocks, owner, count), scalars)
    slots, voxels, rays = weights.shape
    parts = spread.shape[0]
    tiles = total.shape[0] - 1
    half = rays // 2
    rows, cols, slices = relaxed.shape
    total[...] = jnp.zeros_like(total)
    for p in range(parts // 2):
        spread[relative_block(orders[0], p), :half] = a_low[p]
        spread[relative_block(orders[0], p + parts // 2), :half] = a_high[p]
        spread[relative_block(orders[1], p), half:] = b_low[p]
        spread[relative_block(orders[1], p + parts // 2), half:] = b_high[p]

    for copy in lists:
        copy.wait()

    def step(group, carry):
        for k in range(BACKWARD_GROUP):
            s = group * BACKWARD_GROUP + k
            to = jnp.where(s < count[0], tile_ids[s], tiles)
            total[to] += jnp.dot(
                weights[s], spread[owner[blocks[s]] ^ me], preferred_element_type=jnp.float32
            )
        return carry

    lax.fori_loop(0, slots // BACKWARD_GROUP, step, 0)
    for t in range(tiles):
        span = slice(t * TILE, (t + 1) * TILE)
        update = total[t].reshape(rows, TILE, slices)
        relaxed[:, span, :] = jnp.maximum(image[:, span, :] + relax_step * update, 0.0)
    even = lax.rem(me, 2) == 0
    for side, start in (
        (to_near, jnp.where(even, rows - SWEEPS, 0)),
        (to_far, jnp.where(even, 0, rows - SWEEPS)),
    ):
        for i in range(SWEEPS):
            side[i * cols : (i + 1) * cols] = relaxed[start + i].astype(jnp.bfloat16)
    for i in range(rows):
        across = relaxed[i].T
        strip[i] = jnp.where(cut == 0, across[slices - EDGE :], across[:EDGE])


def shifted(x, axis, by):
    size = x.shape[axis]
    place = lax.broadcasted_iota(jnp.int32, x.shape, axis)
    if by > 0:
        return jnp.where(place == 0, 0.0, pltpu.roll(x, 1, axis))
    return jnp.where(place == size - 1, 0.0, pltpu.roll(x, size - 1, axis))


def flows(cell, below):
    rise_rows = below - cell
    rise_inner = shifted(cell, 0, -1) - cell
    rise_outer = shifted(cell, 1, -1) - cell
    scale = lax.rsqrt(
        smooth_square + rise_rows * rise_rows + rise_inner * rise_inner + rise_outer * rise_outer
    )
    return rise_rows * scale, rise_inner * scale, rise_outer * scale


def advance(cell, below, before):
    flow_rows, flow_inner, flow_outer = flows(cell, below)
    diverge = flow_rows - before
    diverge = diverge + (flow_inner - shifted(flow_inner, 0, 1))
    diverge = diverge + (flow_outer - shifted(flow_outer, 1, 1))
    return cell + flow_step * diverge, flow_rows


def patched(rows, strips, cut):
    slices = rows[0].shape[1]
    low_side = cut == 0
    lane = lax.broadcasted_iota(jnp.int32, rows[0].shape, 1)
    first = jnp.where(low_side, slices - SWEEPS, 0)
    patch = (lane >= first) & (lane < first + SWEEPS)
    gap = jnp.zeros((slices - 2 * EDGE, strips.shape[2]), strips.dtype)
    result = []
    for i, row in enumerate(rows):
        across = jnp.concatenate([strips[i, EDGE:], gap, strips[i, :EDGE]], axis=0)
        result.append(jnp.where(patch, across.T, row))
    return result


def inner_kernel(relaxed, strip, *refs):
    rows = relaxed.shape[0]
    result, saves, fields = refs[0], refs[1:3], refs[3:5]
    for field, start in zip(fields, (relaxed, strip)):
        field[...] = start[...]
    for k in range(SWEEPS):
        for field, save in zip(fields, saves):
            save[k, 0:2] = field[k : k + 2]
            save[k, 2:4] = field[rows - 2 - k : rows - k]

        def body(i, before):
            after = []
            for field, flow in zip(fields, before):
                field[i], flow = advance(field[i], field[i + 1], flow)
                after.append(flow)
            return tuple(after)

        before = tuple(flows(field[k], field[k + 1])[0] for field in fields)
        lax.fori_loop(k + 1, rows - 1 - k, body, before, unroll=3)
    inner = [fields[0][i] for i in range(SWEEPS, rows - SWEEPS)]
    strips = fields[1][SWEEPS : rows - SWEEPS]
    for i, row in enumerate(patched(inner, strips, lax.axis_index("cuts"))):
        result[i] = row


def edge_kernel(
    inner, saved, saved_strip, from_near, from_far, volume,
    low_field, low_strip, high_field, high_strip, ends, sems, *, planes,
):
    rows, cols, slices = volume.shape
    me, cut = lax.axis_index("plane"), lax.axis_index("cuts")
    inner_copy = pltpu.make_async_copy(inner, volume.at[pl.ds(SWEEPS, rows - 2 * SWEEPS)], sems.at[0])
    inner_copy.start()
    body_rows = SWEEPS * cols
    even = lax.rem(me, 2) == 0
    for other, this, field, strip, at in (
        (from_near, from_far, low_field, low_strip, (slice(0, 4),)),
        (from_far, from_near, high_field, high_strip, (0, slice(2, 6))),
    ):
        halo = jnp.where(even, this[...], other[...])
        field[at] = halo[:body_rows].astype(jnp.float32).reshape(SWEEPS, cols, slices)
        strip[at] = halo[body_rows:].astype(jnp.float32).reshape(SWEEPS, 2 * EDGE, cols)
    pairs = ((low_field, high_field, saved), (low_strip, high_strip, saved_strip))
    for k in range(SWEEPS):
        now, later = k % 2, (k + 1) % 2
        for low, high, save in pairs:
            low[4:6] = save[k, 0:2]
            high[now, 0:2] = save[k, 2:4]

        @pl.when(me == 0)
        def _():
            for low, _, _ in pairs:
                low[3 - k] = low[4 - k]

        @pl.when(me == planes - 1)
        def _():
            for _, high, _ in pairs:
                high[now, 2 + k] = jnp.zeros(high.shape[2:], high.dtype)

        def body(i, before):
            after = []
            for (low, high, _), (flow_low, flow_high) in zip(pairs, before):
                low[i - 1], flow_low = advance(low[i], low[i + 1], flow_low)
                high[later, i + 1], flow_high = advance(high[now, i], high[now, i + 1], flow_high)
                after.append((flow_low, flow_high))
            return tuple(after)

        before = tuple(
            (flows(low[0], low[1])[0], flows(high[now, 0], high[now, 1])[0]) for low, high, _ in pairs
        )
        lax.fori_loop(1, SWEEPS + 1, body, before, unroll=2)
    last = SWEEPS % 2
    outer = [low_field[i] for i in range(SWEEPS)] + [high_field[last, 2 + i] for i in range(SWEEPS)]
    strips = jnp.concatenate([low_strip[0:4], high_strip[last, 2:6]], axis=0)
    for i, row in enumerate(patched(outer, strips, cut)):
        ends[i] = row
    copies = [
        inner_copy,
        pltpu.make_async_copy(ends.at[pl.ds(0, SWEEPS)], volume.at[pl.ds(0, SWEEPS)], sems.at[1]),
        pltpu.make_async_copy(ends.at[pl.ds(SWEEPS, SWEEPS)], volume.at[pl.ds(rows - SWEEPS, SWEEPS)], sems.at[2]),
    ]
    for copy in copies[1:]:
        copy.start()
    for copy in copies:
        copy.wait()


def partner(bit, planes):
    return [(i, i ^ (1 << bit)) for i in range(planes)]


def sum_chain(keep, send, order, planes):
    for bit in order[:-1]:
        got = lax.ppermute(send, "plane", partner(bit, planes))
        total = keep + got.astype(jnp.float32)
        left = total.shape[0] // 2
        keep, send = total[:left], total[left:].astype(jnp.bfloat16)
    return total, lax.ppermute(total.astype(jnp.bfloat16), "plane", partner(order[-1], planes))


def spread_chain(piece, order, planes):
    for bit in reversed(order[1:-1]):
        got = lax.ppermute(piece, "plane", partner(bit, planes))
        piece = jnp.concatenate([piece, got], axis=0)
    return piece, lax.ppermute(piece, "plane", partner(order[0], planes))


def per_device(
    image,
    projection_weight_tiles,
    pair_tile_index,
    pair_ray_block,
    ray_owner,
    active_pair_count,
    measured,
):
    rows, cols, slices = image.shape
    slots, voxels, rays = projection_weight_tiles.shape
    tiles = (rows // TILE) * (cols // TILE)
    planes = lax.axis_size("plane")
    parts = ray_owner.shape[0]
    half = rays // 2
    bits = planes.bit_length() - 1
    plain = tuple(range(bits))
    swapped = (1, 0) + plain[2:]
    orders = (plain, swapped)
    cut = lax.axis_index("cuts")
    shape = jax.ShapeDtypeStruct
    f32, bf16 = jnp.float32, jnp.bfloat16

    weights = pltpu.with_memory_space_constraint(projection_weight_tiles, pltpu.HBM)
    lists = [
        pltpu.with_memory_space_constraint(a, pltpu.HBM)
        for a in (pair_tile_index, pair_ray_block, ray_owner)
    ] + [active_pair_count]
    far_image = pltpu.with_memory_space_constraint(image, pltpu.HBM)
    scalars = [
        *(pltpu.SMEM(a.shape, jnp.int32) for a in lists),
        pltpu.SemaphoreType.DMA((4,)),
    ]

    kept, sent = shape((parts // 2, slices, half), f32), shape((parts // 2, slices, half), bf16)
    a_keep, a_send, b_keep, b_send, held, pixels = pl.pallas_call(
        functools.partial(forward_kernel, orders),
        out_shape=(kept, sent, kept, sent, shape(weights.shape, bf16), shape(image.shape, f32)),
        in_specs=[HBM] * 6,
        out_specs=(VMEM,) * 6,
        scratch_shapes=[
            pltpu.VMEM((tiles, slices, voxels), bf16),
            pltpu.VMEM((parts + 1, slices, rays), f32),
            pltpu.SemaphoreType.DMA((tiles,)),
            pltpu.SemaphoreType.DMA((slots // FETCH,)),
            *scalars,
        ],
        compiler_params=PARAMS,
        name="forward",
    )(*lists, far_image, weights)

    b_keep, target = lax.optimization_barrier((b_keep, measured))
    pieces = []
    for low, keep, send, order in ((0, a_keep, a_send, plain), (half, b_keep, b_send, swapped)):
        target_other = lax.ppermute(target[:, low : low + half], "plane", partner(order[-1], planes))
        total, got = sum_chain(keep, send, order, planes)
        pieces.append(
            pl.pallas_call(
                functools.partial(residual_kernel, low),
                out_shape=shape((2, half, slices), bf16),
                in_specs=[VMEM] * 4,
                out_specs=VMEM,
                compiler_params=PARAMS,
                name="residual",
            )(total, got, measured, target_other)
        )
    residual = jnp.concatenate([piece[:1] for piece in pieces], axis=1)
    a_low, a_high = spread_chain(pieces[0], plain, planes)
    b_low, b_high = spread_chain(pieces[1], swapped, planes)

    relaxed, to_near, to_far, strip = pl.pallas_call(
        functools.partial(backward_kernel, orders),
        out_shape=(
            shape((rows, cols, slices), f32),
            shape((SWEEPS * cols, slices), bf16),
            shape((SWEEPS * cols, slices), bf16),
            shape((rows, EDGE, cols), f32),
        ),
        in_specs=[HBM] * 4 + [VMEM] * 6,
        out_specs=(VMEM,) * 4,
        scratch_shapes=[
            pltpu.VMEM((parts, rays, slices), bf16),
            pltpu.VMEM((tiles + 1, voxels, slices), f32),
            *scalars,
        ],
        compiler_params=PARAMS,
        name="backward",
    )(*lists, a_low, a_high, b_low, b_high, pixels, held)

    other = lax.ppermute(strip, "cuts", [(0, 1), (1, 0)])
    both = jnp.where(
        cut == 0, jnp.concatenate([strip, other], 1), jnp.concatenate([other, strip], 1)
    )

    even = lax.rem(lax.axis_index("plane"), 2) == 0
    ends = both[rows - SWEEPS :], both[:SWEEPS]

    def trade(main, end_even, end_odd, pairs):
        end = jnp.where(even, end_even, end_odd).astype(bf16).reshape(-1, cols)
        return lax.ppermute(jnp.concatenate([main, end], axis=0), "plane", pairs)

    near = [(i, i ^ 1) for i in range(planes)]
    far = [(i, i + 1 if i % 2 else i - 1) for i in range(1, planes - 1)]
    from_far = trade(to_far, ends[1], ends[0], far)
    from_near = trade(to_near, ends[0], ends[1], near)

    spans = (cols, slices), (2 * EDGE, cols)
    inner, saved, saved_strip = pl.pallas_call(
        inner_kernel,
        out_shape=[
            shape((rows - 2 * SWEEPS, cols, slices), f32),
            *(shape((SWEEPS, 4, *span), f32) for span in spans),
        ],
        in_specs=[VMEM] * 2,
        out_specs=[VMEM] * 3,
        scratch_shapes=[pltpu.VMEM((rows, *span), f32) for span in spans],
        compiler_params=PARAMS,
        name="inner_sweeps",
    )(relaxed, both)
    volume = pl.pallas_call(
        functools.partial(edge_kernel, planes=planes),
        out_shape=shape((rows, cols, slices), f32),
        in_specs=[VMEM] * 5,
        out_specs=HBM,
        scratch_shapes=[
            *(pltpu.VMEM((6, *span), f32) for span in spans),
            *(pltpu.VMEM((2, 6, *span), f32) for span in spans),
            pltpu.VMEM((2 * SWEEPS, cols, slices), f32),
            pltpu.SemaphoreType.DMA((3,)),
        ],
        compiler_params=PARAMS,
        name="edge_sweeps",
    )(inner, saved, saved_strip, from_near, from_far)
    return (volume, residual)


def solution(mesh):
    placed = (
        P("plane", None, "cuts"),
        P("plane", None, None),
        P("plane"),
        P("plane"),
        P(),
        P("plane"),
        P("plane", None, "cuts"),
    )
    return jax.shard_map(
        per_device,
        mesh=mesh,
        in_specs=placed,
        out_specs=(P("plane", None, "cuts"), P("plane", None, "cuts")),
        check_vma=False,
    )
```

```python
import functools

import jax
import jax.numpy as jnp
from jax import lax
from jax.experimental import pallas as pl
from jax.experimental.pallas import tpu as pltpu
from jax.sharding import PartitionSpec as P

TILE = 16
SWEEPS = 4
EDGE = 8
FETCH = 8
FORWARD_GROUP = 16
BACKWARD_GROUP = 96

smooth_square = 0.09
flow_step = 0.04
relax_step = 4.0

VMEM = pl.BlockSpec(memory_space=pltpu.VMEM)
HBM = pl.BlockSpec(memory_space=pltpu.HBM)
PARAMS = pltpu.CompilerParams(vmem_limit_bytes=24 * 1024 * 1024)


def relative_block(bits, position):
    block = 0
    for stage, bit in enumerate(bits):
        block |= ((position >> (len(bits) - 1 - stage)) & 1) << bit
    return block


def weight_copy(weights, held, sems, group):
    span = pl.ds(group * FETCH, FETCH)
    return pltpu.make_async_copy(weights.at[span], held.at[span], sems.at[group])


def list_copies(lists, scalars):
    held, sem = scalars[:-1], scalars[-1]
    copies = [pltpu.make_async_copy(a, b, sem.at[i]) for i, (a, b) in enumerate(zip(lists, held))]
    for copy in copies:
        copy.start()
    return copies, held


def forward_kernel(
    orders, tile_ids, blocks, owner, count, image, weights,
    a_keep, a_send, b_keep, b_send, held, pixels, turned, total, image_sems, sems, *scalars,
):
    me = lax.axis_index("plane")
    lists, (tile_ids, blocks, owner, count) = list_copies((tile_ids, blocks, owner, count), scalars)
    slots, voxels, rays = held.shape
    parts = total.shape[0] - 1
    half = rays // 2
    tiles = turned.shape[0]
    image_copies = []
    for t in range(tiles):
        part = (slice(None), pl.ds(t * TILE, TILE))
        copy = pltpu.make_async_copy(image.at[part], pixels.at[part], image_sems.at[t])
        copy.start(priority=0)
        image_copies.append(copy)
    for fetch in range(12):
        weight_copy(weights, held, sems, fetch).start(priority=1)
    total[...] = jnp.zeros_like(total)
    for copy in image_copies:
        copy.wait()
    for fetch in range(12, slots // FETCH):
        weight_copy(weights, held, sems, fetch).start(priority=1)
    for t in range(tiles):
        tile = pixels[:, t * TILE : (t + 1) * TILE, :].reshape(voxels, pixels.shape[2])
        turned[t] = tile.T.astype(jnp.bfloat16)
    for copy in lists:
        copy.wait()

    def step(group, carry):
        for fetch in range(FORWARD_GROUP // FETCH):
            weight_copy(weights, held, sems, group * (FORWARD_GROUP // FETCH) + fetch).wait()
        for k in range(FORWARD_GROUP):
            s = group * FORWARD_GROUP + k
            to = jnp.where(s < count[0], owner[blocks[s]] ^ me, parts)
            total[to] += jnp.dot(
                turned[tile_ids[s]], held[s], preferred_element_type=jnp.float32
            )
        return carry

    lax.fori_loop(0, slots // FORWARD_GROUP, step, 0)
    for keep, send, order, low in ((a_keep, a_send, orders[0], 0), (b_keep, b_send, orders[1], half)):
        for p in range(parts // 2):
            keep[p] = total[relative_block(order, p), :, low : low + half]
            send[p] = total[relative_block(order, p + parts // 2), :, low : low + half].astype(jnp.bfloat16)


def residual_kernel(low, total, got, measured, measured_other, residual):
    half = residual.shape[1]
    for p, target in enumerate((measured[0, low : low + half, :], measured_other[0])):
        projection = (total[p] + got[1 - p].astype(jnp.float32)).T
        mismatch = target - projection
        residual[p] = (mismatch / jnp.sqrt(1.0 + mismatch * mismatch)).astype(jnp.bfloat16)


def backward_kernel(
    orders, tile_ids, blocks, owner, count, a_low, a_high, b_low, b_high, image, weights,
    relaxed, to_near, to_far, strip, spread, total, *scalars,
):
    me = lax.axis_index("plane")
    cut = lax.axis_index("cuts")
    lists, (tile_ids, blocks, owner, count) = list_copies((tile_ids, blocks, owner, count), scalars)
    slots, voxels, rays = weights.shape
    parts = spread.shape[0]
    tiles = total.shape[0] - 1
    half = rays // 2
    rows, cols, slices = relaxed.shape
    total[...] = jnp.zeros_like(total)
    for p in range(parts // 2):
        spread[relative_block(orders[0], p), :half] = a_low[p]
        spread[relative_block(orders[0], p + parts // 2), :half] = a_high[p]
        spread[relative_block(orders[1], p), half:] = b_low[p]
        spread[relative_block(orders[1], p + parts // 2), half:] = b_high[p]

    for copy in lists:
        copy.wait()

    def step(group, carry):
        for k in range(BACKWARD_GROUP):
            s = group * BACKWARD_GROUP + k
            to = jnp.where(s < count[0], tile_ids[s], tiles)
            total[to] += jnp.dot(
                weights[s], spread[owner[blocks[s]] ^ me], preferred_element_type=jnp.float32
            )
        return carry

    lax.fori_loop(0, slots // BACKWARD_GROUP, step, 0)
    for t in range(tiles):
        span = slice(t * TILE, (t + 1) * TILE)
        update = total[t].reshape(rows, TILE, slices)
        relaxed[:, span, :] = jnp.maximum(image[:, span, :] + relax_step * update, 0.0)
    even = lax.rem(me, 2) == 0
    for side, start in (
        (to_near, jnp.where(even, rows - SWEEPS, 0)),
        (to_far, jnp.where(even, 0, rows - SWEEPS)),
    ):
        for i in range(SWEEPS):
            side[i * cols : (i + 1) * cols] = relaxed[start + i].astype(jnp.bfloat16)
    for i in range(rows):
        across = relaxed[i].T
        strip[i] = jnp.where(cut == 0, across[slices - EDGE :], across[:EDGE])


def shifted(x, axis, by):
    size = x.shape[axis]
    place = lax.broadcasted_iota(jnp.int32, x.shape, axis)
    if by > 0:
        return jnp.where(place == 0, 0.0, pltpu.roll(x, 1, axis))
    return jnp.where(place == size - 1, 0.0, pltpu.roll(x, size - 1, axis))


def flows(cell, below):
    rise_rows = below - cell
    rise_inner = shifted(cell, 0, -1) - cell
    rise_outer = shifted(cell, 1, -1) - cell
    scale = lax.rsqrt(
        smooth_square + rise_rows * rise_rows + rise_inner * rise_inner + rise_outer * rise_outer
    )
    return rise_rows * scale, rise_inner * scale, rise_outer * scale


def advance(cell, below, before):
    flow_rows, flow_inner, flow_outer = flows(cell, below)
    diverge = flow_rows - before
    diverge = diverge + (flow_inner - shifted(flow_inner, 0, 1))
    diverge = diverge + (flow_outer - shifted(flow_outer, 1, 1))
    return cell + flow_step * diverge, flow_rows


def patched(rows, strips, cut):
    slices = rows[0].shape[1]
    low_side = cut == 0
    lane = lax.broadcasted_iota(jnp.int32, rows[0].shape, 1)
    first = jnp.where(low_side, slices - SWEEPS, 0)
    patch = (lane >= first) & (lane < first + SWEEPS)
    gap = jnp.zeros((slices - 2 * EDGE, strips.shape[2]), strips.dtype)
    result = []
    for i, row in enumerate(rows):
        across = jnp.concatenate([strips[i, EDGE:], gap, strips[i, :EDGE]], axis=0)
        result.append(jnp.where(patch, across.T, row))
    return result


def inner_kernel(relaxed, strip, *refs):
    rows = relaxed.shape[0]
    result, saves, fields = refs[0], refs[1:3], refs[3:5]
    for field, start in zip(fields, (relaxed, strip)):
        field[...] = start[...]
    for k in range(SWEEPS):
        for field, save in zip(fields, saves):
            save[k, 0:2] = field[k : k + 2]
            save[k, 2:4] = field[rows - 2 - k : rows - k]

        def body(i, before):
            after = []
            for field, flow in zip(fields, before):
                field[i], flow = advance(field[i], field[i + 1], flow)
                after.append(flow)
            return tuple(after)

        before = tuple(flows(field[k], field[k + 1])[0] for field in fields)
        lax.fori_loop(k + 1, rows - 1 - k, body, before, unroll=3)
    inner = [fields[0][i] for i in range(SWEEPS, rows - SWEEPS)]
    strips = fields[1][SWEEPS : rows - SWEEPS]
    for i, row in enumerate(patched(inner, strips, lax.axis_index("cuts"))):
        result[i] = row


def edge_kernel(
    inner, saved, saved_strip, from_near, ends_near, from_far, volume,
    low_field, low_strip, high_field, high_strip, finished, sems, *, planes,
):
    rows, cols, slices = volume.shape
    me, cut = lax.axis_index("plane"), lax.axis_index("cuts")
    inner_copy = pltpu.make_async_copy(inner, volume.at[pl.ds(SWEEPS, rows - 2 * SWEEPS)], sems.at[0])
    inner_copy.start()
    body_rows = SWEEPS * cols
    even = lax.rem(me, 2) == 0
    for far_side, field, strip, at in (
        (even, low_field, low_strip, (slice(0, 4),)),
        (~even, high_field, high_strip, (0, slice(2, 6))),
    ):
        halo = jnp.where(far_side, from_far[:body_rows], from_near[...])
        ends = jnp.where(far_side, from_far[body_rows:], ends_near[...])
        field[at] = halo.astype(jnp.float32).reshape(SWEEPS, cols, slices)
        strip[at] = ends.astype(jnp.float32).reshape(SWEEPS, 2 * EDGE, cols)
    pairs = ((low_field, high_field, saved), (low_strip, high_strip, saved_strip))
    for k in range(SWEEPS):
        now, later = k % 2, (k + 1) % 2
        for low, high, save in pairs:
            low[4:6] = save[k, 0:2]
            high[now, 0:2] = save[k, 2:4]

        @pl.when(me == 0)
        def _():
            for low, _, _ in pairs:
                low[3 - k] = low[4 - k]

        @pl.when(me == planes - 1)
        def _():
            for _, high, _ in pairs:
                high[now, 2 + k] = jnp.zeros(high.shape[2:], high.dtype)

        def body(i, before):
            after = []
            for (low, high, _), (flow_low, flow_high) in zip(pairs, before):
                low[i - 1], flow_low = advance(low[i], low[i + 1], flow_low)
                high[later, i + 1], flow_high = advance(high[now, i], high[now, i + 1], flow_high)
                after.append((flow_low, flow_high))
            return tuple(after)

        before = tuple(
            (flows(low[0], low[1])[0], flows(high[now, 0], high[now, 1])[0]) for low, high, _ in pairs
        )
        lax.fori_loop(1, SWEEPS + 1, body, before, unroll=2)
    last = SWEEPS % 2
    outer = [low_field[i] for i in range(SWEEPS)] + [high_field[last, 2 + i] for i in range(SWEEPS)]
    strips = jnp.concatenate([low_strip[0:4], high_strip[last, 2:6]], axis=0)
    copies = [inner_copy]
    for i, row in enumerate(patched(outer, strips, cut)):
        finished[i] = row
        place = i if i < SWEEPS else rows - 2 * SWEEPS + i
        copies.append(pltpu.make_async_copy(finished.at[i], volume.at[place], sems.at[1 + i]))
        copies[-1].start()
    for copy in copies:
        copy.wait()


def partner(bit, planes):
    return [(i, i ^ (1 << bit)) for i in range(planes)]


def sum_chain(keep, send, order, planes):
    for bit in order[:-1]:
        got = lax.ppermute(send, "plane", partner(bit, planes))
        total = keep + got.astype(jnp.float32)
        left = total.shape[0] // 2
        keep, send = total[:left], total[left:].astype(jnp.bfloat16)
    return total, lax.ppermute(total.astype(jnp.bfloat16), "plane", partner(order[-1], planes))


def spread_chain(piece, order, planes):
    for bit in reversed(order[1:-1]):
        got = lax.ppermute(piece, "plane", partner(bit, planes))
        piece = jnp.concatenate([piece, got], axis=0)
    return piece, lax.ppermute(piece, "plane", partner(order[0], planes))


def per_device(
    image,
    projection_weight_tiles,
    pair_tile_index,
    pair_ray_block,
    ray_owner,
    active_pair_count,
    measured,
):
    rows, cols, slices = image.shape
    slots, voxels, rays = projection_weight_tiles.shape
    tiles = (rows // TILE) * (cols // TILE)
    planes = lax.axis_size("plane")
    parts = ray_owner.shape[0]
    half = rays // 2
    bits = planes.bit_length() - 1
    plain = tuple(range(bits))
    swapped = (1, 0) + plain[2:]
    orders = (plain, swapped)
    cut = lax.axis_index("cuts")
    shape = jax.ShapeDtypeStruct
    f32, bf16 = jnp.float32, jnp.bfloat16

    weights = pltpu.with_memory_space_constraint(projection_weight_tiles, pltpu.HBM)
    lists = [
        pltpu.with_memory_space_constraint(a, pltpu.HBM)
        for a in (pair_tile_index, pair_ray_block, ray_owner)
    ] + [active_pair_count]
    far_image = pltpu.with_memory_space_constraint(image, pltpu.HBM)
    scalars = [
        *(pltpu.SMEM(a.shape, jnp.int32) for a in lists),
        pltpu.SemaphoreType.DMA((4,)),
    ]

    kept, sent = shape((parts // 2, slices, half), f32), shape((parts // 2, slices, half), bf16)
    a_keep, a_send, b_keep, b_send, held, pixels = pl.pallas_call(
        functools.partial(forward_kernel, orders),
        out_shape=(kept, sent, kept, sent, shape(weights.shape, bf16), shape(image.shape, f32)),
        in_specs=[HBM] * 6,
        out_specs=(VMEM,) * 6,
        scratch_shapes=[
            pltpu.VMEM((tiles, slices, voxels), bf16),
            pltpu.VMEM((parts + 1, slices, rays), f32),
            pltpu.SemaphoreType.DMA((tiles,)),
            pltpu.SemaphoreType.DMA((slots // FETCH,)),
            *scalars,
        ],
        compiler_params=PARAMS,
        name="forward",
    )(*lists, far_image, weights)

    b_keep, target = lax.optimization_barrier((b_keep, measured))
    pieces = []
    for low, keep, send, order in ((0, a_keep, a_send, plain), (half, b_keep, b_send, swapped)):
        target_other = lax.ppermute(target[:, low : low + half], "plane", partner(order[-1], planes))
        total, got = sum_chain(keep, send, order, planes)
        pieces.append(
            pl.pallas_call(
                functools.partial(residual_kernel, low),
                out_shape=shape((2, half, slices), bf16),
                in_specs=[VMEM] * 4,
                out_specs=VMEM,
                compiler_params=PARAMS,
                name="residual",
            )(total, got, measured, target_other)
        )
    residual = jnp.concatenate([piece[:1] for piece in pieces], axis=1)
    a_low, a_high = spread_chain(pieces[0], plain, planes)
    b_low, b_high = spread_chain(pieces[1], swapped, planes)

    relaxed, to_near, to_far, strip = pl.pallas_call(
        functools.partial(backward_kernel, orders),
        out_shape=(
            shape((rows, cols, slices), f32),
            shape((SWEEPS * cols, slices), bf16),
            shape((SWEEPS * cols, slices), bf16),
            shape((rows, EDGE, cols), f32),
        ),
        in_specs=[HBM] * 4 + [VMEM] * 6,
        out_specs=(VMEM,) * 4,
        scratch_shapes=[
            pltpu.VMEM((parts, rays, slices), bf16),
            pltpu.VMEM((tiles + 1, voxels, slices), f32),
            *scalars,
        ],
        compiler_params=PARAMS,
        name="backward",
    )(*lists, a_low, a_high, b_low, b_high, pixels, held)

    other = lax.ppermute(strip, "cuts", [(0, 1), (1, 0)])
    both = jnp.where(
        cut == 0, jnp.concatenate([strip, other], 1), jnp.concatenate([other, strip], 1)
    )

    even = lax.rem(lax.axis_index("plane"), 2) == 0
    ends = both[rows - SWEEPS :], both[:SWEEPS]

    def ends_for(end_even, end_odd):
        return jnp.where(even, end_even, end_odd).astype(bf16).reshape(-1, cols)

    near = [(i, i ^ 1) for i in range(planes)]
    far = [(i, i + 1 if i % 2 else i - 1) for i in range(1, planes - 1)]
    from_near = lax.ppermute(to_near, "plane", near)
    from_far = lax.ppermute(
        jnp.concatenate([to_far, ends_for(ends[1], ends[0])], axis=0), "plane", far
    )
    ends_near = lax.ppermute(ends_for(ends[0], ends[1]), "plane", near)

    spans = (cols, slices), (2 * EDGE, cols)
    inner, saved, saved_strip = pl.pallas_call(
        inner_kernel,
        out_shape=[
            shape((rows - 2 * SWEEPS, cols, slices), f32),
            *(shape((SWEEPS, 4, *span), f32) for span in spans),
        ],
        in_specs=[VMEM] * 2,
        out_specs=[VMEM] * 3,
        scratch_shapes=[pltpu.VMEM((rows, *span), f32) for span in spans],
        compiler_params=PARAMS,
        name="inner_sweeps",
    )(relaxed, both)
    volume = pl.pallas_call(
        functools.partial(edge_kernel, planes=planes),
        out_shape=shape((rows, cols, slices), f32),
        in_specs=[VMEM] * 6,
        out_specs=HBM,
        scratch_shapes=[
            *(pltpu.VMEM((6, *span), f32) for span in spans),
            *(pltpu.VMEM((2, 6, *span), f32) for span in spans),
            pltpu.VMEM((2 * SWEEPS, cols, slices), f32),
            pltpu.SemaphoreType.DMA((1 + 2 * SWEEPS,)),
        ],
        compiler_params=PARAMS,
        name="edge_sweeps",
    )(inner, saved, saved_strip, from_near, ends_near, from_far)
    return (volume, residual)


def solution(mesh):
    placed = (
        P("plane", None, "cuts"),
        P("plane", None, None),
        P("plane"),
        P("plane"),
        P(),
        P("plane"),
        P("plane", None, "cuts"),
    )
    return jax.shard_map(
        per_device,
        mesh=mesh,
        in_specs=placed,
        out_specs=(P("plane", None, "cuts"), P("plane", None, "cuts")),
        check_vma=False,
    )
```
